256 devices in a mesh: seq: 64 (over y, z, core), head: 4 (over x).
Axes of the slice: x: 4, y: 4, z: 8, core: 2. Of those that a mesh axis runs over, the one named last changes fastest.
Arguments:
- hidden_in: bfloat16 [8192, 7168], P('seq', 'head'), may hold values from -6 to 6
- w_down: bfloat16 [7168, 2112], P(('head', 'seq')), may hold values from -0.0625 to 0.0625
- q_gain: float32 [1536], replicated, may hold values from 0.5 to 10
- kv_gain: float32 [512], replicated, may hold values from 0.5 to 10
- w_qb: bfloat16 [1536, 6144], P(None, 'head'), may hold values from -0.15625 to 0.15625
- w_uk: bfloat16 [32, 128, 512], P('head'), may hold values from -0.25 to 0.25
- w_uv: bfloat16 [32, 512, 128], P('head'), may hold values from -0.25 to 0.25
- cache_pool: bfloat16 [512, 64, 576], P('seq'), may hold values from -6 to 6
- hit_owner: int32 [64, 27], replicated, may hold values from 0 to 63, as said below
- hit_block: int32 [64, 27], replicated, may hold values from 0 to 7
- hit_count: int32 [64], replicated, may hold values from 25 to 27, as said below
Outputs:
- attended: bfloat16 [8192, 4096], P('seq', 'head')
The draws below stay inside these ranges and needn't reach their ends.
Inputs may be any that keep to these rules, and one draw needn't show every extreme that they name: `hit_owner`: each span's 27 slots name different owners. `hit_count`: some span has all 27 slots live, some only 27 - max(1, 2).
All inputs are finite; a program needn't handle non-finite values.
Results may differ from the reference program's by a relative error of at most 0.035.
The reference program's roundings to bfloat16 on the way (of `q_norm`, `latent`, `query`, `q_full` and `rounded`) count: a program that leaves them out, or rounds other values in their place, can miss the bound.
Values may be sent and summed in bfloat16 or wider, within the bound.
No kernel may reach another device: no remote copies, remote signals or barrier semaphores. Data moves between devices by JAX's collectives and lax.ppermute only.
A program may use at most 128 MiB of HBM per device.

```python
import math
import jax
import jax.numpy as jnp
from jax import lax

D = 7168
QL = 1536
KL = 512
RD = 64
ND = 128
VD = 128
HEADS = 32
CH = 128
BLK = 64
PB = 8
SPANS = 64
HMAX = 27
L = 8192
POOL = 512


def draw_q_gain(key, part):
    key = jax.random.fold_in(key, 13)
    return jax.random.uniform(key, (QL,), jnp.float32, 0.5, 1.5)


def draw_kv_gain(key, part):
    key = jax.random.fold_in(key, 14)
    return jax.random.uniform(key, (KL,), jnp.float32, 0.5, 1.5)


def draw_hit_owner(key, part):
    key = jax.random.fold_in(key, 11)
    keys = jax.random.split(key, SPANS)
    rows = jax.vmap(lambda single: jax.random.permutation(single, SPANS))(keys)
    return rows[:, :HMAX].astype(jnp.int32)


def draw_hit_count(key, part):
    key = jax.random.fold_in(key, 12)
    first_key, second_key = jax.random.split(key)
    drop = max(1, HMAX // 10)
    counts = HMAX - jax.random.randint(first_key, (SPANS,), 0, drop + 1)
    order = jax.random.permutation(second_key, SPANS)
    counts = counts.at[order[0]].set(HMAX)
    counts = counts.at[order[1]].set(HMAX - drop)
    return counts.astype(jnp.int32)


def plant(drawn, stream_key, least, largest):
    longest = drawn.shape.index(max(drawn.shape))
    spots = []
    for shift in (0, 1):
        where = [jax.random.randint(jax.random.fold_in(stream_key, axis), (), 0, length) for axis, length in enumerate(drawn.shape)]
        where[longest] = (where[longest] + shift) % drawn.shape[longest]
        spots.append(tuple(where))
    return drawn.at[spots[0]].set(least).at[spots[1]].set(largest)


def steps_of(stream_key, dims, cuts, smallest, high):
    level, own = 1.0, jax.random.fold_in(stream_key, 6)
    for dim, shards_of in cuts:
        steps = jnp.exp(jax.random.uniform(jax.random.fold_in(own, dim), (shards_of,), jnp.float32, smallest / len(cuts), high / len(cuts)))
        level = level * jnp.repeat(steps, dims[dim] // shards_of).reshape([-1 if axis == dim else 1 for axis in range(len(dims))])
    return level


def gaussian(key, dims, spread, most, pieces=(), kind=jnp.bfloat16):
    drawn = spread * jax.random.normal(key, dims, jnp.float32)
    if pieces:
        drawn = drawn * steps_of(key, dims, pieces, -0.22, 0.18)
    return jnp.clip(drawn, -most, most).astype(kind)


def setup_inputs(seed: int = 0) -> dict:
    key_of = jax.random.split(jax.random.key(seed), 12)
    return {
        "hidden_in": gaussian(key_of[0], (L, D), 1.0, 6.0, ((0, 64), (1, 4))),
        "w_down": gaussian(key_of[1], (D, QL + KL + RD), D ** -0.5, 0.0625, ((0, 256),)),
        "q_gain": draw_q_gain(jax.random.fold_in(key_of[11], 71), 0),
        "kv_gain": draw_kv_gain(jax.random.fold_in(key_of[11], 71), 0),
        "w_qb": gaussian(key_of[4], (QL, HEADS * (ND + RD)), QL ** -0.5, 0.15625, ((1, 4),)),
        "w_uk": gaussian(key_of[5], (HEADS, ND, KL), KL ** -0.5, 0.25, ((0, 4),)),
        "w_uv": gaussian(key_of[6], (HEADS, KL, VD), KL ** -0.5, 0.25, ((0, 4),)),
        "cache_pool": gaussian(key_of[7], (POOL, BLK, KL + RD), 1.0, 6.0, ((0, 64),)),
        "hit_owner": draw_hit_owner(jax.random.fold_in(key_of[11], 71), 0),
        "hit_block": plant(jax.random.randint(key_of[9], (SPANS, HMAX), 0, PB), jax.random.fold_in(key_of[9], 1), 0, PB - 1).astype(jnp.int32),
        "hit_count": draw_hit_count(jax.random.fold_in(key_of[11], 71), 0),
    }


ROPE_BASE = 50000.0
EPS = 1e-06

def normalize(vec):
    return vec * lax.rsqrt(lax.optimization_barrier(jnp.mean(vec * vec, axis=-1, keepdims=True)) + EPS)

def rotate(vec, positions):
    half = vec.shape[-1] // 2
    freqs = ROPE_BASE ** (-jnp.arange(half, dtype=jnp.float32) / half)
    angles = positions.astype(jnp.float32)[:, None] * freqs[None, :]
    if vec.ndim == 3:
        angles = angles[:, None, :]
    cosine = jnp.cos(angles)
    sine = jnp.sin(angles)
    first = vec[..., :half]
    second = vec[..., half:]
    return jnp.concatenate([first * cosine - second * sine, second * cosine + first * sine], axis=-1)

def prepare(projected, positions, q_gain, kv_gain, w_qb, w_uk):
    rows = projected.shape[0]
    q_norm = (normalize(projected[:, :QL]) * q_gain).astype(jnp.bfloat16)
    c_lat = (normalize(projected[:, QL:QL + KL]) * kv_gain).astype(jnp.bfloat16)
    k_rope = rotate(projected[:, QL + KL:], positions).astype(jnp.bfloat16)
    latent = jnp.concatenate([c_lat, k_rope], axis=1)
    heads = w_qb.shape[1] // (ND + RD)
    query = jnp.dot(q_norm, w_qb, preferred_element_type=jnp.float32).astype(jnp.bfloat16)
    query = query.reshape(rows, heads, ND + RD)
    absorbed = jnp.einsum('rhn,hnc->rhc', query[:, :, :ND].astype(jnp.float32), w_uk.astype(jnp.float32))
    q_rope = rotate(query[:, :, ND:].astype(jnp.float32), positions)
    q_full = jnp.concatenate([absorbed, q_rope], axis=2).astype(jnp.bfloat16)
    return (latent, q_full)

def reference(hidden_in, w_down, q_gain, kv_gain, w_qb, w_uk, w_uv, cache_pool, hit_owner, hit_block, hit_count):
    projected = jnp.dot(hidden_in, w_down, preferred_element_type=jnp.float32)
    positions = jnp.arange(L, dtype=jnp.int32)
    latent, q_full = prepare(projected, positions, q_gain, kv_gain, w_qb, w_uk)
    scale = 1.0 / math.sqrt(ND + RD)
    slots = jnp.arange(HMAX, dtype=jnp.int32)
    stretch_pos = jnp.arange(L, dtype=jnp.int32)
    value_up = w_uv.astype(jnp.float32)

    def one_span(index):
        queries = lax.dynamic_slice_in_dim(q_full, index * CH, CH, 0).astype(jnp.float32)
        query_pos = index * CH + jnp.arange(CH, dtype=jnp.int32)
        ids = hit_owner[index] * PB + hit_block[index]
        prefix = cache_pool[ids].reshape(HMAX * BLK, KL + RD)
        keys = jnp.concatenate([prefix, latent], axis=0).astype(jnp.float32)
        prefix_ok = jnp.repeat(slots < hit_count[index], BLK)
        stretch_ok = stretch_pos[None, :] <= query_pos[:, None]
        allowed = jnp.concatenate([jnp.broadcast_to(prefix_ok[None, :], (CH, HMAX * BLK)), stretch_ok], axis=1)
        scores = jnp.einsum('rhc,kc->rhk', queries, keys) * scale
        scores = jnp.where(allowed[:, None, :], scores, -jnp.inf)
        best = lax.optimization_barrier(jnp.max(scores, axis=2, keepdims=True))
        weights = jnp.exp(scores - best)
        total = lax.optimization_barrier(jnp.sum(weights, axis=2))
        rounded = lax.optimization_barrier(weights.astype(jnp.bfloat16)).astype(jnp.float32)
        mixed = jnp.einsum('rhk,kc->rhc', rounded, keys[:, :KL]) / total[:, :, None]
        outcome = jnp.einsum('rhc,hcv->rhv', mixed, value_up, precision=lax.Precision.HIGHEST)
        return outcome.reshape(CH, -1)
    result = lax.map(one_span, jnp.arange(SPANS, dtype=jnp.int32))
    return result.reshape(L, -1).astype(jnp.bfloat16)
```

```python
import functools
import math

import jax
import jax.numpy as jnp
from jax import lax
from jax.experimental import pallas as pl
from jax.experimental.pallas import tpu as pltpu
from jax.sharding import Mesh, PartitionSpec as P

QL = 1536
KL = 512
RD = 64
ND = 128
VD = 128
WIDTH = KL + RD
COLS = QL + KL + RD
CH = 128
BLK = 64
HMAX = 27
NY, NZ, NC, NX = 4, 8, 2, 4
QUART = CH // NX
SPAN_AXES = ("y", "z", "c")

ROPE_BASE = 50000.0
EPS = 1e-06
NEGATIVE = -1e30
LOG2 = math.log2(math.e) / math.sqrt(ND + RD)
FAR = 1 << 20
F32 = jnp.float32
BF16 = jnp.bfloat16
MIB = 1 << 20
WHOLE = pl.BlockSpec(memory_space=pltpu.VMEM)
SCALARS = pl.BlockSpec(memory_space=pltpu.SMEM)


def shift(value, axis, size, by):
    return lax.ppermute(value, axis, [(i, (i + by) % size) for i in range(size)])


def ring_four(block, axis):
    half = block.shape[0] // 2
    up = shift(block, axis, 4, 1)
    down = shift(block, axis, 4, -1)
    return {
        0: block,
        1: up,
        -1: down,
        2: (shift(up[:half], axis, 4, 1), shift(down[half:], axis, 4, -1)),
    }


def ring_eight(block, axis):
    half = block.shape[0] // 2
    out = {0: block}
    up = down = block
    for step in (1, 2, 3):
        up = shift(up, axis, 8, 1)
        down = shift(down, axis, 8, -1)
        out[step] = up
        out[-step] = down
    out[4] = (shift(up[:half], axis, 8, 1), shift(down[half:], axis, 8, -1))
    return out


def flat(block):
    return jnp.concatenate(block) if isinstance(block, tuple) else block


def rope_tables(positions):
    half = RD // 2
    freqs = ROPE_BASE ** (-jnp.arange(half, dtype=F32) / half)
    angles = positions.astype(F32)[:, None] * freqs[None, :]
    cosine = jnp.cos(angles)
    sine = jnp.sin(angles)
    return (
        jnp.concatenate([cosine, cosine], axis=1),
        jnp.concatenate([-sine, sine], axis=1),
    )


def rotate(vec, cosine, sine):
    half = RD // 2
    swapped = jnp.concatenate([vec[:, half:], vec[:, :half]], axis=1)
    return vec * cosine + swapped * sine


def choose_kernel(wanted_ref, start_ref, pool_ref, out_ref):
    first = pl.multiple_of(start_ref[0], 16)

    def one(index, carry):
        out_ref[index] = pool_ref[wanted_ref[index], pl.ds(first, BLK // NX), :]
        return carry

    lax.fori_loop(0, out_ref.shape[0], one, 0)


def choose(wanted, start, pool):
    return pl.pallas_call(
        choose_kernel,
        out_shape=jax.ShapeDtypeStruct((wanted.shape[0], BLK // NX, WIDTH), BF16),
        in_specs=[SCALARS, SCALARS, WHOLE],
        out_specs=WHOLE,
        compiler_params=pltpu.CompilerParams(vmem_limit_bytes=8 * MIB),
        cost_estimate=pl.CostEstimate(flops=0, bytes_accessed=2 * MIB, transcendentals=0),
        name="choose",
    )(wanted, start, pool)


def norm_kernel(parts_ref, q_gain_ref, kv_gain_ref, cos_ref, sin_ref, out_ref, row_ref):
    groups = NY * NC
    wide = COLS // groups
    for group in range(groups):
        total = parts_ref[group * NX]
        for other in range(1, NX):
            total = total + parts_ref[group * NX + other]
        row_ref[:, group * wide : (group + 1) * wide] = total
    query = row_ref[:, :QL]
    scale = lax.rsqrt(jnp.mean(query * query, axis=1, keepdims=True) + EPS)
    out_ref[:, :QL] = (query * scale * q_gain_ref[...]).astype(BF16)
    key = row_ref[:, QL : QL + KL]
    scale = lax.rsqrt(jnp.mean(key * key, axis=1, keepdims=True) + EPS)
    out_ref[:, QL : QL + KL] = (key * scale * kv_gain_ref[...]).astype(BF16)
    rope = rotate(row_ref[:, QL + KL :], cos_ref[...], sin_ref[...])
    out_ref[:, QL + KL :] = rope.astype(BF16)


def norm(parts, q_gain, kv_gain, cosine, sine):
    return pl.pallas_call(
        norm_kernel,
        out_shape=jax.ShapeDtypeStruct((QUART, COLS), BF16),
        in_specs=[WHOLE] * 5,
        out_specs=WHOLE,
        scratch_shapes=[pltpu.VMEM((QUART, COLS), F32)],
        compiler_params=pltpu.CompilerParams(vmem_limit_bytes=8 * MIB),
        name="norm",
    )(parts, q_gain, kv_gain, cosine, sine)


def query_kernel(norm_ref, w_ref, up_ref, cos_ref, sin_ref, out_ref):
    query = jnp.dot(norm_ref[...], w_ref[...], preferred_element_type=F32).astype(BF16)
    for pair in range(2):
        base = pair * (ND + RD)
        lifted = jnp.dot(
            query[:, base : base + ND], up_ref[pair], preferred_element_type=F32
        )
        out_ref[pair, :, :KL] = lifted.astype(BF16)
        rope = query[:, base + ND : base + ND + RD].astype(F32)
        out_ref[pair, :, KL:] = rotate(rope, cos_ref[...], sin_ref[...]).astype(BF16)


def queries(q_norm, w_qb, w_uk, cosine, sine):
    heads = w_uk.shape[0]
    rows = q_norm.shape[0]
    wide = 2 * (ND + RD)
    return pl.pallas_call(
        query_kernel,
        out_shape=jax.ShapeDtypeStruct((heads, rows, WIDTH), BF16),
        grid=(heads // 2,),
        in_specs=[
            pl.BlockSpec((rows, QL), lambda i: (0, 0)),
            pl.BlockSpec((QL, wide), lambda i: (0, i)),
            pl.BlockSpec((2, ND, KL), lambda i: (i, 0, 0)),
            pl.BlockSpec((rows, RD), lambda i: (0, 0)),
            pl.BlockSpec((rows, RD), lambda i: (0, 0)),
        ],
        out_specs=pl.BlockSpec((2, rows, WIDTH), lambda i: (i, 0, 0)),
        compiler_params=pltpu.CompilerParams(vmem_limit_bytes=16 * MIB),
        cost_estimate=pl.CostEstimate(
            flops=2 * rows * QL * QL, bytes_accessed=7 * MIB, transcendentals=0
        ),
        name="queries",
    )(q_norm, w_qb, w_uk, cosine, sine)


def flash_kernel(size, group, first, last, *refs):
    flags_ref, base_ref, q_ref, k_ref, pos_ref = refs[:5]
    refs = refs[5:]
    if first:
        top_in = sum_in = acc_in = None
    else:
        top_in, sum_in, acc_in = refs[:3]
        refs = refs[3:]
    if last:
        w_ref, out_ref, top_ref, sum_ref, acc_ref = refs
    else:
        top_ref, sum_ref, acc_ref = refs
    rows = q_ref.shape[0]
    if first:
        top_ref[...] = jnp.full(top_ref.shape, NEGATIVE, F32)
        sum_ref[...] = jnp.zeros(sum_ref.shape, F32)
        acc_ref[...] = jnp.zeros(acc_ref.shape, F32)
    else:
        top_ref[...] = top_in[...]
        sum_ref[...] = sum_in[...]
        acc_ref[...] = acc_in[...]

    def step(index, masked):
        keys = k_ref[pl.ds(pl.multiple_of(index * size, 16), size), :]
        for start in range(0, rows, group):
            part = pl.ds(start, group)
            scores = lax.dot_general(
                q_ref[part, :], keys, (((1,), (1,)), ((), ())), preferred_element_type=F32
            )
            if masked:
                token = lax.broadcasted_iota(jnp.int32, (group, 1), 0) & (CH - 1)
                seen = pos_ref[index] <= token + base_ref[0]
                scores = jnp.where(seen, scores, NEGATIVE)
            before = top_ref[part, :]
            top = jnp.maximum(before, jnp.max(scores, axis=1, keepdims=True))
            weights = jnp.exp2((scores - top) * LOG2)
            shrink = jnp.exp2((before - top) * LOG2)
            top_ref[part, :] = top
            sum_ref[part, :] = sum_ref[part, :] * shrink + jnp.sum(
                weights, axis=1, keepdims=True
            )
            acc_ref[part, :] = acc_ref[part, :] * shrink + jnp.dot(
                weights.astype(BF16), keys[:, :KL], preferred_element_type=F32
            )

    def block(index, carry):
        flag = flags_ref[index]

        @pl.when(flag == 1)
        def _():
            step(index, False)

        @pl.when(flag == 2)
        def _():
            step(index, True)

        return carry

    lax.fori_loop(0, k_ref.shape[0] // size, block, 0)
    if last:
        for head in range(rows // CH):
            part = pl.ds(head * CH, CH)
            mixed = acc_ref[part, :] / sum_ref[part, :]
            high = mixed.astype(BF16)
            low = (mixed - high.astype(F32)).astype(BF16)
            weight = w_ref[head]
            lifted = jnp.dot(high, weight, preferred_element_type=F32)
            lifted = lifted + jnp.dot(low, weight, preferred_element_type=F32)
            out_ref[:, head * VD : (head + 1) * VD] = lifted.astype(BF16)


def flash(query, keys, positions, base, size, state=None, w_uv=None, group=256):
    rows = query.shape[0]
    blocks = keys.shape[0] // size
    positions = positions.reshape(blocks, 1, size)
    lowest = jnp.min(positions, axis=(1, 2))
    highest = jnp.max(positions, axis=(1, 2))
    flags = jnp.where(highest <= base, 1, jnp.where(lowest > base + CH - 1, 0, 2))
    first, last = state is None, w_uv is not None
    shapes = [
        jax.ShapeDtypeStruct((rows, 1), F32),
        jax.ShapeDtypeStruct((rows, 1), F32),
        jax.ShapeDtypeStruct((rows, KL), F32),
    ]
    operands = [flags.astype(jnp.int32), base.reshape(1), query, keys, positions]
    specs = [SCALARS, SCALARS, WHOLE, WHOLE, WHOLE]
    if not first:
        operands += list(state)
        specs += [WHOLE] * 3
    scratch = []
    if last:
        operands.append(w_uv)
        specs.append(WHOLE)
        scratch = [pltpu.VMEM(s.shape, s.dtype) for s in shapes]
        shapes = [jax.ShapeDtypeStruct((CH, rows // CH * VD), BF16)]
    out = pl.pallas_call(
        functools.partial(flash_kernel, size, group, first, last),
        out_shape=shapes,
        in_specs=specs,
        out_specs=[WHOLE] * len(shapes),
        scratch_shapes=scratch,
        compiler_params=pltpu.CompilerParams(vmem_limit_bytes=40 * MIB),
        cost_estimate=pl.CostEstimate(
            flops=2 * rows * keys.shape[0] * (WIDTH + KL),
            bytes_accessed=8 * MIB,
            transcendentals=rows * keys.shape[0],
        ),
        name="flash",
    )(*operands)
    return out[0] if last else tuple(out)


def body(
    hidden_in,
    w_down,
    q_gain,
    kv_gain,
    w_qb,
    w_uk,
    w_uv,
    cache_pool,
    hit_owner,
    hit_block,
    hit_count,
):
    y = lax.axis_index("y")
    z = lax.axis_index("z")
    c = lax.axis_index("c")
    x = lax.axis_index("x")
    span = (y * NZ + z) * NC + c
    base = (span * CH).astype(jnp.int32)
    rows = hidden_in.shape[0]
    heads = w_uk.shape[0]
    feats = hidden_in.shape[1]
    parts = NY * NC
    per = w_down.shape[0]
    wide = COLS // parts

    pieces = w_down.reshape(per, parts, wide).transpose(1, 0, 2)
    pieces = lax.all_to_all(pieces, ("y", "c"), 0, 0, tiled=True).reshape(parts * per, wide)
    down = lax.all_gather(pieces, "z", axis=0, tiled=True)
    pair = NC * per
    hidden = hidden_in.reshape(rows, NY, NZ, pair).transpose(0, 2, 1, 3).reshape(rows, feats)
    mine = jnp.zeros((NY, rows, feats), BF16)
    for by in range(NY):
        block = shift(hidden, "y", NY, by) if by else hidden
        mine = lax.dynamic_update_slice(mine, block[None], ((y - by) % NY, 0, 0))
    theirs = shift(mine, "c", NC, 1)
    even = c == 0
    tokens = jnp.stack(
        [jnp.where(even, mine, theirs), jnp.where(even, theirs, mine)], axis=1
    ).reshape(parts * rows, feats)
    partial_proj = jnp.dot(tokens, down, preferred_element_type=F32)
    arrived = lax.all_to_all(partial_proj, ("y", "c", "x"), 0, 0, tiled=True)

    cosine, sine = rope_tables(base + jnp.arange(rows, dtype=jnp.int32))
    quarter = lambda table: lax.dynamic_slice_in_dim(table, x * QUART, QUART, 0)
    normed = norm(
        arrived.reshape(parts * NX, QUART, wide),
        q_gain[None, :],
        kv_gain[None, :],
        quarter(cosine),
        quarter(sine),
    )
    normed = lax.all_gather(normed, "x", axis=0, tiled=True)
    latent = normed[:, QL:]
    query = queries(normed[:, :QL], w_qb, w_uk, cosine, sine).reshape(heads * rows, WIDTH)

    live = jnp.arange(HMAX, dtype=jnp.int32)[None, :] < hit_count[:, None]
    asking = (hit_owner == span) & live
    wanted = jnp.sum(jnp.where(asking, hit_block, 0), axis=1)
    quarter_rows = BLK // NX
    outgoing = choose(wanted, (x * quarter_rows).reshape(1), cache_pool)
    outgoing = outgoing.reshape(-1, WIDTH)
    incoming = lax.all_to_all(outgoing, SPAN_AXES, 0, 0, tiled=True)
    my_owner = lax.dynamic_index_in_dim(hit_owner, span, 0, keepdims=False)
    my_count = lax.dynamic_index_in_dim(hit_count, span, 0, keepdims=False)
    zero = jnp.zeros((1,), jnp.int32)
    prefix = choose(my_owner, zero, incoming.reshape(-1, quarter_rows, WIDTH))
    prefix = prefix.reshape(HMAX * quarter_rows, WIDTH)
    prefix = [flat(block) for block in ring_four(prefix, "x").values()]
    slot = jnp.arange(HMAX * quarter_rows, dtype=jnp.int32) // quarter_rows
    prefix_pos = jnp.tile(jnp.where(slot < my_count, -1, FAR), NX)
    state = flash(query, jnp.concatenate(prefix), prefix_pos, base, HMAX * quarter_rows)

    half = rows // 2
    order_z = (0, 1, -1, 2, -2, 3, -3, 4)
    order_y = (0, 1, -1, 2)
    row = jnp.arange(half, dtype=jnp.int32)

    def places(from_y, from_z, core, part):
        spans = (((y - from_y) % NY) * NZ + (z - from_z) % NZ) * NC + core
        return spans * CH + part * half + row

    lines = ring_eight(latent[:half], "z")
    plane = ring_four(jnp.concatenate([flat(lines[k]) for k in order_z]), "y")
    columns = ring_four(latent[half:], "y")
    stack = ring_eight(jnp.concatenate([flat(columns[k]) for k in order_y]), "z")

    def plane_pos(from_y, core):
        return jnp.concatenate([places(from_y, k, core, 0) for k in order_z])

    def stack_pos(from_z, core):
        return jnp.concatenate([places(k, from_z, core, 1) for k in order_y])

    def both(keys, pos):
        keys = jnp.concatenate(keys) if len(keys) > 1 else keys[0]
        other = shift(keys, "c", NC, 1)
        return jnp.concatenate([keys, other]), jnp.concatenate(pos(c) + pos(1 - c))

    size = 1024
    keys, pos = both([plane[0]], lambda core: [plane_pos(0, core)])
    state = flash(query, keys, pos, base, size, state)
    keys, pos = both(
        [plane[1], plane[-1]], lambda core: [plane_pos(1, core), plane_pos(-1, core)]
    )
    state = flash(query, keys, pos, base, size, state)
    near = (0, 1, -1, 2, -2, 3)
    keys, pos = both([stack[k] for k in near], lambda core: [stack_pos(k, core) for k in near])
    state = flash(query, keys, pos, base, size, state)
    far = (-3, 4)
    keys, pos = both(
        [flat(plane[2])] + [flat(stack[k]) for k in far],
        lambda core: [plane_pos(2, core)] + [stack_pos(k, core) for k in far],
    )
    return flash(query, keys, pos, base, size, state, w_uv)


def solution(mesh):
    fine = Mesh(mesh.devices.reshape(NY, NZ, NC, NX), ("y", "z", "c", "x"))
    span = SPAN_AXES
    in_specs = (
        P(span, "x"),
        P(("x",) + span, None),
        P(),
        P(),
        P(None, "x"),
        P("x", None, None),
        P("x", None, None),
        P(span, None, None),
        P(),
        P(),
        P(),
    )
    return jax.shard_map(
        body, mesh=fine, in_specs=in_specs, out_specs=P(span, "x"), check_vma=False
    )
```

```python
import functools
import math

import jax
import jax.numpy as jnp
from jax import lax
from jax.experimental import pallas as pl
from jax.experimental.pallas import tpu as pltpu
from jax.sharding import Mesh, PartitionSpec as P

QL = 1536
KL = 512
RD = 64
ND = 128
VD = 128
WIDTH = KL + RD
PADDED = 640
COLS = QL + KL + RD
CH = 128
BLK = 64
PB = 8
HMAX = 27
NY, NZ, NC, NX = 4, 8, 2, 4
QUART = CH // NX
HALF = CH // 2
SIXTEENTH = HALF // NX
PIECE = NZ * HALF
SLICE = BLK // NX
GROUP = 256
SPAN_AXES = ("y", "z", "c")

ROPE_BASE = 50000.0
EPS = 1e-06
NEGATIVE = -1e30
LOG2 = math.log2(math.e) / math.sqrt(ND + RD)
F32 = jnp.float32
BF16 = jnp.bfloat16
MIB = 1 << 20
GRANT = 56 * MIB
WHOLE = pl.BlockSpec(memory_space=pltpu.VMEM)
SCALARS = pl.BlockSpec(memory_space=pltpu.SMEM)
OUTSIDE = pl.BlockSpec(memory_space=pl.ANY)


def shift(value, axis, size, by):
    return lax.ppermute(value, axis, [(i, (i + by) % size) for i in range(size)])


def offsets(block, axis, size):
    return [block] + [shift(block, axis, size, by) for by in range(1, size)]


def rope_tables(positions):
    half = RD // 2
    freqs = ROPE_BASE ** (-jnp.arange(half, dtype=F32) / half)
    angles = positions.astype(F32)[:, None] * freqs[None, :]
    cosine = jnp.cos(angles)
    sine = jnp.sin(angles)
    return (
        jnp.concatenate([cosine, cosine], axis=1),
        jnp.concatenate([-sine, sine], axis=1),
    )


def rotate(vec, cosine, sine):
    half = RD // 2
    swapped = jnp.concatenate([vec[:, half:], vec[:, :half]], axis=1)
    return vec * cosine + swapped * sine


def quarter_kernel(x_ref, pool_ref, out_ref):
    first = pl.multiple_of(x_ref[0] * SLICE, SLICE)
    for index in range(pool_ref.shape[0]):
        part = pl.ds(index * SLICE, SLICE)
        out_ref[part, :WIDTH] = pool_ref[index, pl.ds(first, SLICE), :]
        out_ref[part, WIDTH:] = jnp.zeros((SLICE, PADDED - WIDTH), BF16)


def quarter_pool(x, pool):
    return pl.pallas_call(
        quarter_kernel,
        out_shape=jax.ShapeDtypeStruct((pool.shape[0] * SLICE, PADDED), BF16),
        in_specs=[SCALARS, WHOLE],
        out_specs=WHOLE,
        compiler_params=pltpu.CompilerParams(vmem_limit_bytes=8 * MIB),
        name="quarter",
    )(x.reshape(1), pool)


def serve_kernel(place_ref, wanted_ref, pool_in, after_ref, *refs):
    out_refs, (pool_ref, sems) = refs[:NY], refs[NY:]
    move([(pool_in, pool_ref)], sems)
    y, core = place_ref[0], place_ref[2]
    for by, out_ref in enumerate(out_refs):
        line = (y + by) & (NY - 1)
        for other in range(NC):
            side = core if other == 0 else 1 - core
            for index in range(NZ):
                block = wanted_ref[(line * NC + side) * NZ + index]
                row = pl.multiple_of(block * SLICE, SLICE)
                start = (other * NZ + index) * SLICE
                out_ref[pl.ds(start, SLICE), :] = pool_ref[pl.ds(row, SLICE), :]


def serve(place, wanted, pool, after):
    return pl.pallas_call(
        serve_kernel,
        out_shape=[jax.ShapeDtypeStruct((NC * NZ * SLICE, PADDED), BF16)] * NY,
        in_specs=[SCALARS, SCALARS, OUTSIDE, OUTSIDE],
        out_specs=[WHOLE] * NY,
        scratch_shapes=[pltpu.VMEM(pool.shape, BF16), pltpu.SemaphoreType.DMA((1,))],
        compiler_params=pltpu.CompilerParams(vmem_limit_bytes=8 * MIB),
        name="serve",
    )(place, wanted, pool, after)


def sort_kernel(*refs):
    served, (_, mine_ref, give_ref) = refs[:NY], refs[NY:]
    size = NZ * SLICE
    for by, ref in enumerate(served):
        mine_ref[pl.ds(by * size, size), :] = ref[:size, :]
        give_ref[pl.ds(by * size, size), :] = ref[size:, :]


def sort(served, after):
    return pl.pallas_call(
        sort_kernel,
        out_shape=[jax.ShapeDtypeStruct((NY * NZ * SLICE, PADDED), BF16)] * 2,
        in_specs=[WHOLE] * NY + [OUTSIDE],
        out_specs=[WHOLE] * 2,
        compiler_params=pltpu.CompilerParams(vmem_limit_bytes=8 * MIB),
        name="sort",
    )(*served, after)


def pick_kernel(place_ref, owner_ref, mine_ref, theirs_ref, out_ref):
    y, core = place_ref[0], place_ref[2]

    def one(index, carry):
        owner = owner_ref[index]
        line = (y + NY - (owner >> 4)) & (NY - 1)
        row = pl.multiple_of((line * NZ + ((owner >> 1) & (NZ - 1))) * SLICE, SLICE)
        target = pl.ds(pl.multiple_of(index * SLICE, SLICE), SLICE)
        here = (owner & 1) == core

        @pl.when(here)
        def _():
            out_ref[target, :] = mine_ref[pl.ds(row, SLICE), :]

        @pl.when(jnp.logical_not(here))
        def _():
            out_ref[target, :] = theirs_ref[pl.ds(row, SLICE), :]

        return carry

    lax.fori_loop(0, HMAX, one, 0)


def pick(place, owner, mine, theirs):
    return pl.pallas_call(
        pick_kernel,
        out_shape=jax.ShapeDtypeStruct((HMAX * SLICE, PADDED), BF16),
        in_specs=[SCALARS, SCALARS, WHOLE, WHOLE],
        out_specs=WHOLE,
        compiler_params=pltpu.CompilerParams(vmem_limit_bytes=8 * MIB),
        name="pick",
    )(place, owner, mine, theirs)


def norm_kernel(parts_ref, q_gain_ref, kv_gain_ref, cos_ref, sin_ref, after_ref, out_ref, row_ref):
    groups = NY * NC
    wide = COLS // groups
    for group in range(groups):
        total = parts_ref[group * NX]
        for other in range(1, NX):
            total = total + parts_ref[group * NX + other]
        row_ref[:, group * wide : (group + 1) * wide] = total
    query = row_ref[:, :QL]
    scale = lax.rsqrt(jnp.mean(query * query, axis=1, keepdims=True) + EPS)
    out_ref[:, :QL] = (query * scale * q_gain_ref[...]).astype(BF16)
    key = row_ref[:, QL : QL + KL]
    scale = lax.rsqrt(jnp.mean(key * key, axis=1, keepdims=True) + EPS)
    out_ref[:, QL : QL + KL] = (key * scale * kv_gain_ref[...]).astype(BF16)
    rope = rotate(row_ref[:, QL + KL :], cos_ref[...], sin_ref[...])
    out_ref[:, QL + KL :] = rope.astype(BF16)


def norm(parts, q_gain, kv_gain, cosine, sine, after):
    return pl.pallas_call(
        norm_kernel,
        out_shape=jax.ShapeDtypeStruct((QUART, COLS), BF16),
        in_specs=[WHOLE] * 5 + [OUTSIDE],
        out_specs=WHOLE,
        scratch_shapes=[pltpu.VMEM((QUART, COLS), F32)],
        compiler_params=pltpu.CompilerParams(vmem_limit_bytes=8 * MIB),
        name="norm",
    )(parts, q_gain, kv_gain, cosine, sine, after)


def query_kernel(norm_ref, w_ref, up_ref, cos_ref, sin_ref, after_ref, out_ref):
    query = jnp.dot(norm_ref[...], w_ref[...], preferred_element_type=F32).astype(BF16)
    for pair in range(2):
        base = pair * (ND + RD)
        lifted = jnp.dot(
            query[:, base : base + ND], up_ref[pair], preferred_element_type=F32
        )
        out_ref[pair, :, :KL] = lifted.astype(BF16)
        rope = query[:, base + ND : base + ND + RD].astype(F32)
        out_ref[pair, :, KL:WIDTH] = rotate(rope, cos_ref[...], sin_ref[...]).astype(BF16)
        out_ref[pair, :, WIDTH:] = jnp.zeros((out_ref.shape[1], PADDED - WIDTH), BF16)


def queries(q_norm, w_qb, w_uk, cosine, sine, after):
    heads = w_uk.shape[0]
    rows = q_norm.shape[0]
    wide = 2 * (ND + RD)
    return pl.pallas_call(
        query_kernel,
        out_shape=jax.ShapeDtypeStruct((heads, rows, PADDED), BF16),
        grid=(heads // 2,),
        in_specs=[
            pl.BlockSpec((rows, QL), lambda i: (0, 0)),
            pl.BlockSpec((QL, wide), lambda i: (0, i)),
            pl.BlockSpec((2, ND, KL), lambda i: (i, 0, 0)),
            pl.BlockSpec((rows, RD), lambda i: (0, 0)),
            pl.BlockSpec((rows, RD), lambda i: (0, 0)),
            pl.BlockSpec(memory_space=pl.ANY),
        ],
        out_specs=pl.BlockSpec((2, rows, PADDED), lambda i: (i, 0, 0)),
        compiler_params=pltpu.CompilerParams(vmem_limit_bytes=GRANT),
        cost_estimate=pl.CostEstimate(
            flops=2 * rows * QL * QL, bytes_accessed=7 * MIB, transcendentals=0
        ),
        name="queries",
    )(q_norm, w_qb, w_uk, cosine, sine, after)


def move(pairs, sems):
    copies = [
        pltpu.make_async_copy(source, target, sems.at[index])
        for index, (source, target) in enumerate(pairs)
    ]
    for copy in copies:
        copy.start()
    for copy in copies:
        copy.wait()


def stack_kernel(*refs):
    out_ref = refs[-1]
    start = 0
    for ref in refs[:-1]:
        out_ref[pl.ds(start, ref.shape[0]), :] = ref[...]
        start += ref.shape[0]


def stack(*blocks):
    shape = (sum(b.shape[0] for b in blocks), blocks[0].shape[1])
    return pl.pallas_call(
        stack_kernel,
        out_shape=jax.ShapeDtypeStruct(shape, blocks[0].dtype),
        in_specs=[WHOLE] * len(blocks),
        out_specs=WHOLE,
        compiler_params=pltpu.CompilerParams(vmem_limit_bytes=16 * MIB),
        name="stack",
    )(*blocks)


def gate_kernel(*refs):
    del refs


def gate(blocks, after):
    return pl.pallas_call(
        gate_kernel,
        out_shape=[jax.ShapeDtypeStruct(b.shape, b.dtype) for b in blocks],
        in_specs=[OUTSIDE] * (len(blocks) + 1),
        out_specs=[OUTSIDE] * len(blocks),
        input_output_aliases={i: i for i in range(len(blocks))},
        compiler_params=pltpu.CompilerParams(vmem_limit_bytes=4 * MIB),
        name="gate",
    )(*blocks, after)


def project_kernel(place_ref, down_in, *refs):
    count = NY * NC
    blocks, (out_ref, token_ref, down_ref, sems) = refs[:count], refs[count:]
    pairs = [(down_in, down_ref)] + [(ref, token_ref.at[i]) for i, ref in enumerate(blocks)]
    copies = [
        pltpu.make_async_copy(source, target, sems.at[index])
        for index, (source, target) in enumerate(pairs)
    ]
    for copy in copies:
        copy.start()
    y, core = place_ref[0], place_ref[2]
    copies[0].wait()
    for index in range(count):
        copies[index + 1].wait()
        line = (y + NY - index // NC) & (NY - 1)
        side = core if index % NC == 0 else 1 - core
        out_ref[line, side] = jnp.dot(
            token_ref[index], down_ref[...], preferred_element_type=F32
        )


def project(place, blocks, down):
    rows = blocks[0].shape[0]
    return pl.pallas_call(
        project_kernel,
        out_shape=jax.ShapeDtypeStruct((NY, NC, rows, down.shape[1]), F32),
        in_specs=[SCALARS] + [OUTSIDE] * (len(blocks) + 1),
        out_specs=WHOLE,
        scratch_shapes=[
            pltpu.VMEM((len(blocks),) + blocks[0].shape, BF16),
            pltpu.VMEM(down.shape, BF16),
            pltpu.SemaphoreType.DMA((len(blocks) + 1,)),
        ],
        compiler_params=pltpu.CompilerParams(vmem_limit_bytes=GRANT),
        name="project",
    )(place, down, *blocks)


def spread_kernel(place_ref, normed_ref, send_ref):
    x = place_ref[3]
    send_ref[:, WIDTH:] = jnp.zeros((send_ref.shape[0], PADDED - WIDTH), BF16)
    send_ref[:HALF, :WIDTH] = normed_ref[:HALF, QL:]
    first = pl.multiple_of(HALF + x * SIXTEENTH, SIXTEENTH)
    send_ref[HALF:, :WIDTH] = normed_ref[pl.ds(first, SIXTEENTH), QL:]


def spread(place, normed):
    return pl.pallas_call(
        spread_kernel,
        out_shape=jax.ShapeDtypeStruct((HALF + SIXTEENTH, PADDED), BF16),
        in_specs=[SCALARS, WHOLE],
        out_specs=WHOLE,
        compiler_params=pltpu.CompilerParams(vmem_limit_bytes=8 * MIB),
        name="spread",
    )(place, normed)


def split_kernel(line_ref, whole_ref, piece_ref):
    both = HALF + SIXTEENTH
    for index in range(NZ):
        start = index * both
        whole_ref[pl.ds(index * HALF, HALF), :] = line_ref[pl.ds(start, HALF), :]
        piece_ref[pl.ds(index * SIXTEENTH, SIXTEENTH), :] = line_ref[
            pl.ds(start + HALF, SIXTEENTH), :
        ]


def split(line):
    return pl.pallas_call(
        split_kernel,
        out_shape=[
            jax.ShapeDtypeStruct((NZ * HALF, PADDED), BF16),
            jax.ShapeDtypeStruct((NZ * SIXTEENTH, PADDED), BF16),
        ],
        in_specs=[WHOLE],
        out_specs=[WHOLE] * 2,
        compiler_params=pltpu.CompilerParams(vmem_limit_bytes=8 * MIB),
        name="split",
    )(line)


def fold(state, query_at, key_ref, rows, first, seen_at):
    top_ref, sum_ref, acc_ref = state

    def score(start):
        return lax.dot_general(
            query_at(start), key_ref[...], (((1,), (1,)), ((), ())), preferred_element_type=F32
        )

    ready = score(0)
    for start in range(0, rows, GROUP):
        scores = ready
        if start + GROUP < rows:
            ready = score(start + GROUP)
        if seen_at is not None:
            scores = jnp.where(seen_at(), scores, NEGATIVE)
        part = pl.ds(pl.multiple_of(first + start, GROUP), GROUP)
        before = top_ref[part, :]
        top = jnp.maximum(before, jnp.max(scores, axis=1, keepdims=True))
        weights = jnp.exp2((scores - top) * LOG2)
        shrink = jnp.exp2((before - top) * LOG2)
        top_ref[part, :] = top
        sum_ref[part, :] = sum_ref[part, :] * shrink + jnp.sum(weights, axis=1, keepdims=True)
        acc_ref[part, :] = acc_ref[part, :] * shrink + jnp.dot(
            weights.astype(BF16), key_ref[:, :KL], preferred_element_type=F32
        )


def lift(side, w_ref, out_ref, top_ref, sum_ref, acc_ref):
    heads = w_ref.shape[0]
    for head in range(heads):
        part = pl.ds((side * heads + head) * CH, CH)
        mixed = acc_ref[part, :]
        high = mixed.astype(BF16)
        low = (mixed - high.astype(F32)).astype(BF16)
        weight = w_ref[head]
        lifted = jnp.dot(high, weight, preferred_element_type=F32)
        lifted = lifted + jnp.dot(low, weight, preferred_element_type=F32)
        out_ref[:, head * VD : (head + 1) * VD] = lifted
        at = heads * VD + head
        out_ref[:, at : at + 1] = top_ref[part, :]
        out_ref[:, at + heads : at + heads + 1] = sum_ref[part, :]


def prefix_kernel(place_ref, q_ref, key_in, w_ref, out_ref, *scratch):
    top_ref, sum_ref, acc_ref, live_ref, key_ref, sems = scratch
    state = (top_ref, sum_ref, acc_ref)
    rows = q_ref.shape[0]
    top_ref[...] = jnp.full(top_ref.shape, NEGATIVE, F32)
    sum_ref[...] = jnp.zeros(sum_ref.shape, F32)
    acc_ref[...] = jnp.zeros(acc_ref.shape, F32)
    size = key_ref.shape[0] // NX
    slot = lax.broadcasted_iota(jnp.int32, (1, size), 1) // SLICE
    live = jnp.where(slot < place_ref[4], 1, 0)
    for index in range(NX):
        live_ref[:, index * size : (index + 1) * size] = live
    move([(key_in, key_ref)], sems)
    query_at = lambda start: q_ref[start : start + GROUP, :]
    fold(state, query_at, key_ref, rows, 0, lambda: live_ref[...] > 0)
    lift(0, w_ref, out_ref, top_ref, sum_ref, acc_ref)


def state_scratch(rows):
    return [
        pltpu.VMEM((rows, 1), F32),
        pltpu.VMEM((rows, 1), F32),
        pltpu.VMEM((rows, KL), F32),
    ]


def lifted_shape(w_uv):
    return jax.ShapeDtypeStruct((CH, w_uv.shape[0] * VD + CH), F32)


def prefix_pass(place, query, keys, w_uv):
    rows = query.shape[0]
    return pl.pallas_call(
        prefix_kernel,
        out_shape=lifted_shape(w_uv),
        in_specs=[SCALARS, WHOLE, OUTSIDE, WHOLE],
        out_specs=WHOLE,
        scratch_shapes=state_scratch(rows)
        + [
            pltpu.VMEM((1, keys.shape[0]), jnp.int32),
            pltpu.VMEM(keys.shape, BF16),
            pltpu.SemaphoreType.DMA((1,)),
        ],
        compiler_params=pltpu.CompilerParams(vmem_limit_bytes=GRANT),
        cost_estimate=pl.CostEstimate(
            flops=2 * rows * keys.shape[0] * (WIDTH + KL),
            bytes_accessed=8 * MIB,
            transcendentals=rows * keys.shape[0],
        ),
        name="prefix",
    )(place, query, keys, w_uv)


def stretch_kernel(kinds, place_ref, q_ref, *refs):
    pieces, refs = refs[: len(kinds)], refs[len(kinds) :]
    w_ref, _, keep_ref, give_ref, top_ref, sum_ref, acc_ref, key_ref, pos_ref, sems = refs
    copies = []
    for index, ((kind, by), ref) in enumerate(zip(kinds, pieces)):
        if kind == "line" and by:
            line = (place_ref[0] + NY - by) & (NY - 1)
            ref = ref.at[pl.ds(pl.multiple_of(line * PIECE, PIECE), PIECE), :]
        target = key_ref.at[pl.ds(index * PIECE, PIECE), :]
        copies.append(pltpu.make_async_copy(ref, target, sems.at[index]))
        copies[-1].start()
    top_ref[...] = jnp.full(top_ref.shape, NEGATIVE, F32)
    sum_ref[...] = jnp.zeros(sum_ref.shape, F32)
    acc_ref[...] = jnp.zeros(acc_ref.shape, F32)
    y, z, core, x = (place_ref[i] for i in range(4))
    lane = lax.broadcasted_iota(jnp.int32, (1, PIECE), 1)
    full, empty = [], []
    for index, (kind, by) in enumerate(kinds):
        if kind == "line":
            line = (y + NY - by) & (NY - 1)
            pos = ((line * NZ + (lane >> 6)) * NC + core) * CH + (lane & (HALF - 1))
            full.append(line < y)
            empty.append(line > y)
        else:
            line = (y + NY - (lane >> 7)) & (NY - 1)
            token = HALF + SIXTEENTH * ((x + NX - by) & (NX - 1)) + (lane & (SIXTEENTH - 1))
            pos = ((line * NZ + ((lane >> 4) & (NZ - 1))) * NC + core) * CH + token
            full.append(jnp.bool_(False))
            empty.append(jnp.bool_(False))
        pos_ref[:, index * PIECE : (index + 1) * PIECE] = pos
    rows = q_ref.shape[0] // 2
    span = (y * NZ + z) * NC + core
    for copy in copies:
        copy.wait()
    is_full = functools.reduce(jnp.logical_and, full)
    is_empty = functools.reduce(jnp.logical_and, empty)

    def block(side, carry):
        base = (span + side * (1 - 2 * core)) * CH

        def run(masked):
            def query_at(start):
                return q_ref[pl.ds(pl.multiple_of(side * rows + start, GROUP), GROUP), :]

            def seen():
                token = lax.broadcasted_iota(jnp.int32, (GROUP, 1), 0) & (CH - 1)
                return pos_ref[...] <= token + base

            state = (top_ref, sum_ref, acc_ref)
            fold(state, query_at, key_ref, rows, side * rows, seen if masked else None)

        @pl.when(is_full)
        def _():
            run(False)

        @pl.when(jnp.logical_not(is_full | is_empty))
        def _():
            run(True)

        return carry

    lax.fori_loop(0, NC, block, 0)
    lift(0, w_ref, keep_ref, top_ref, sum_ref, acc_ref)
    lift(1, w_ref, give_ref, top_ref, sum_ref, acc_ref)


def stretch_pass(place, query, pieces, w_uv, after):
    rows = query.shape[0]
    kinds = tuple(piece[:2] for piece in pieces)
    arrays = [piece[2] for piece in pieces]
    keys = len(kinds) * PIECE
    operands = [place, query, *arrays, w_uv, after]
    return pl.pallas_call(
        functools.partial(stretch_kernel, kinds),
        out_shape=[lifted_shape(w_uv)] * 2,
        in_specs=[SCALARS, WHOLE] + [OUTSIDE] * len(kinds) + [WHOLE, OUTSIDE],
        out_specs=[WHOLE] * 2,
        scratch_shapes=state_scratch(rows)
        + [
            pltpu.VMEM((keys, PADDED), BF16),
            pltpu.VMEM((1, keys), jnp.int32),
            pltpu.SemaphoreType.DMA((len(kinds),)),
        ],
        compiler_params=pltpu.CompilerParams(vmem_limit_bytes=GRANT),
        cost_estimate=pl.CostEstimate(
            flops=2 * rows * keys * (WIDTH + KL),
            bytes_accessed=8 * MIB,
            transcendentals=rows * keys,
        ),
        name="stretch",
    )(*operands)


def merge_kernel(*refs):
    parts, out_ref = refs[:-1], refs[-1]
    heads = out_ref.shape[1] // VD
    for head in range(heads):
        at = heads * VD + head
        tops = [ref[:, at : at + 1] for ref in parts]
        top = functools.reduce(jnp.maximum, tops)
        total = mixed = 0.0
        for ref, own in zip(parts, tops):
            scale = jnp.exp2((own - top) * LOG2)
            total = total + ref[:, at + heads : at + heads + 1] * scale
            mixed = mixed + ref[:, head * VD : (head + 1) * VD] * scale
        out_ref[:, head * VD : (head + 1) * VD] = (mixed / total).astype(BF16)


def merge(parts):
    return pl.pallas_call(
        merge_kernel,
        out_shape=jax.ShapeDtypeStruct((CH, parts[0].shape[1] - CH), BF16),
        in_specs=[WHOLE] * len(parts),
        out_specs=WHOLE,
        compiler_params=pltpu.CompilerParams(vmem_limit_bytes=12 * MIB),
        name="merge",
    )(*parts)


def body(
    hidden_in,
    w_down,
    q_gain,
    kv_gain,
    w_qb,
    w_uk,
    w_uv,
    cache_pool,
    hit_owner,
    hit_block,
    hit_count,
):
    y = lax.axis_index("y").astype(jnp.int32)
    z = lax.axis_index("z").astype(jnp.int32)
    c = lax.axis_index("c").astype(jnp.int32)
    x = lax.axis_index("x").astype(jnp.int32)
    span = (y * NZ + z) * NC + c
    my_owner = lax.dynamic_index_in_dim(hit_owner, span, 0, keepdims=False)
    my_count = lax.dynamic_index_in_dim(hit_count, span, 0, keepdims=False)
    place = jnp.stack([y, z, c, x, my_count])
    rows = hidden_in.shape[0]
    heads = w_uk.shape[0]
    feats = hidden_in.shape[1]
    parts = NY * NC
    per = w_down.shape[0]
    wide = COLS // parts
    cosine, sine = rope_tables(span * CH + jnp.arange(rows, dtype=jnp.int32))
    quarter = lambda table: lax.dynamic_slice_in_dim(table, x * QUART, QUART, 0)

    pair = NC * per
    hidden = hidden_in.reshape(rows, NY, NZ, pair).transpose(0, 2, 1, 3).reshape(rows, feats)
    pieces = w_down.reshape(per, parts, wide).transpose(1, 0, 2)
    pieces = lax.all_to_all(pieces, ("y", "c"), 0, 0, tiled=True).reshape(parts * per, wide)
    down = lax.all_gather(pieces, "z", axis=0, tiled=True)
    (hidden,) = gate([hidden], pieces)
    others = gate(offsets(hidden, "y", NY)[1:], down)
    tokens = []
    for block in [hidden, *others]:
        tokens += [block, shift(block, "c", NC, 1)]

    pool = lax.all_gather(quarter_pool(x, cache_pool), "z", axis=0, tiled=True)
    table = lambda array: lax.dynamic_index_in_dim(
        array.reshape(NY, NZ, NC, -1), z, 1, keepdims=False
    )
    live = jnp.arange(HMAX, dtype=jnp.int32) < table(hit_count)
    owners = (y * NZ + jnp.arange(NZ, dtype=jnp.int32)) * NC + c
    asking = (table(hit_owner) == owners[:, None, None, None]) & live
    wanted = jnp.sum(jnp.where(asking, table(hit_block), 0), axis=3)
    wanted = wanted + PB * jnp.arange(NZ, dtype=jnp.int32)[:, None, None]
    wanted = jnp.transpose(wanted, (1, 2, 0)).reshape(-1)
    served = serve(place, wanted, pool, down)
    partial_proj = project(place, tokens, down).reshape(parts * rows, wide)
    arrived = lax.all_to_all(partial_proj, ("y", "c", "x"), 0, 0, tiled=True)
    ours, give = sort([served[0]] + [shift(served[by], "y", NY, by) for by in range(1, NY)], arrived)
    prefix = pick(place, my_owner, ours, shift(give, "c", NC, 1))
    prefix_all = lax.all_gather(prefix, "x", axis=0, tiled=True)

    normed = norm(
        arrived.reshape(parts * NX, QUART, wide),
        q_gain[None, :],
        kv_gain[None, :],
        quarter(cosine),
        quarter(sine),
        prefix,
    )
    normed = lax.all_gather(normed, "x", axis=0, tiled=True)
    send = spread(place, normed)

    whole, piece = split(lax.all_gather(send, "z", axis=0, tiled=True))
    piece = stack(*offsets(piece, "y", NY))
    lines = lax.all_gather(whole, "y", axis=0, tiled=True)
    planes = offsets(piece, "x", NX)

    query = queries(normed, w_qb, w_uk, cosine, sine, whole).reshape(heads * rows, PADDED)
    query_all = stack(query, shift(query, "c", NC, 1))

    parts = [prefix_pass(place, query, prefix_all, w_uv)]
    for pieces in (
        [("line", 0, whole), ("plane", 0, planes[0]), ("line", 1, lines), ("line", 2, lines)],
        [
            ("plane", 1, planes[1]),
            ("plane", 3, planes[3]),
            ("line", 3, lines),
            ("plane", 2, planes[2]),
        ],
    ):
        keep, give = stretch_pass(place, query_all, pieces, w_uv, parts[-2] if parts[1:] else parts[0])
        parts += [keep, shift(give, "c", NC, 1)]
    return merge(parts)


def solution(mesh):
    fine = Mesh(mesh.devices.reshape(NY, NZ, NC, NX), ("y", "z", "c", "x"))
    span = SPAN_AXES
    in_specs = (
        P(span, "x"),
        P(("x",) + span, None),
        P(),
        P(),
        P(None, "x"),
        P("x", None, None),
        P("x", None, None),
        P(span, None, None),
        P(),
        P(),
        P(),
    )
    return jax.shard_map(
        body, mesh=fine, in_specs=in_specs, out_specs=P(span, "x"), check_vma=False
    )
```

```python
import functools
import math

import jax
import jax.numpy as jnp
from jax import lax
from jax.experimental import pallas as pl
from jax.experimental.pallas import tpu as pltpu
from jax.sharding import Mesh, PartitionSpec as P

QL = 1536
KL = 512
RD = 64
ND = 128
VD = 128
WIDTH = KL + RD
PADDED = 640
COLS = QL + KL + RD
CH = 128
BLK = 64
PB = 8
HMAX = 27
LEAST = 25
NY, NZ, NC, NX = 4, 8, 2, 4
QUART = CH // NX
HALF = CH // 2
SIXTEENTH = HALF // NX
PIECE = NZ * HALF
SLICE = BLK // NX
GROUP = 256
SPAN_AXES = ("y", "z", "c")

ROPE_BASE = 50000.0
EPS = 1e-06
NEGATIVE = -1e30
LOG2 = math.log2(math.e) / math.sqrt(ND + RD)
F32 = jnp.float32
BF16 = jnp.bfloat16
MIB = 1 << 20
GRANT = 56 * MIB
WHOLE = pl.BlockSpec(memory_space=pltpu.VMEM)
SCALARS = pl.BlockSpec(memory_space=pltpu.SMEM)
OUTSIDE = pl.BlockSpec(memory_space=pl.ANY)


def shift(value, axis, size, by):
    return lax.ppermute(value, axis, [(i, (i + by) % size) for i in range(size)])


def offsets(block, axis, size):
    return [block] + [shift(block, axis, size, by) for by in range(1, size)]


def rope_tables(positions):
    half = RD // 2
    freqs = ROPE_BASE ** (-jnp.arange(half, dtype=F32) / half)
    angles = positions.astype(F32)[:, None] * freqs[None, :]
    cosine = jnp.cos(angles)
    sine = jnp.sin(angles)
    return (
        jnp.concatenate([cosine, cosine], axis=1),
        jnp.concatenate([-sine, sine], axis=1),
    )


def rotate(vec, cosine, sine):
    half = RD // 2
    swapped = jnp.concatenate([vec[:, half:], vec[:, :half]], axis=1)
    return vec * cosine + swapped * sine


def quarter_kernel(x_ref, pool_ref, out_ref):
    first = pl.multiple_of(x_ref[0] * SLICE, SLICE)
    for index in range(pool_ref.shape[0]):
        part = pl.ds(index * SLICE, SLICE)
        out_ref[part, :WIDTH] = pool_ref[index, pl.ds(first, SLICE), :]
        out_ref[part, WIDTH:] = jnp.zeros((SLICE, PADDED - WIDTH), BF16)


def quarter_pool(x, pool):
    return pl.pallas_call(
        quarter_kernel,
        out_shape=jax.ShapeDtypeStruct((pool.shape[0] * SLICE, PADDED), BF16),
        in_specs=[SCALARS, WHOLE],
        out_specs=WHOLE,
        compiler_params=pltpu.CompilerParams(vmem_limit_bytes=8 * MIB),
        name="quarter",
    )(x.reshape(1), pool)


def serve_kernel(place_ref, wanted_ref, pool_in, after_ref, *refs):
    out_refs, (pool_ref, sems) = refs[:NY], refs[NY:]
    move([(pool_in, pool_ref)], sems)
    y, core = place_ref[0], place_ref[2]
    for by, out_ref in enumerate(out_refs):
        line = (y + by) & (NY - 1)
        for other in range(NC):
            side = core if other == 0 else 1 - core
            for index in range(NZ):
                block = wanted_ref[(line * NC + side) * NZ + index]
                row = pl.multiple_of(block * SLICE, SLICE)
                start = (other * NZ + index) * SLICE
                out_ref[pl.ds(start, SLICE), :] = pool_ref[pl.ds(row, SLICE), :]


def serve(place, wanted, pool, after):
    return pl.pallas_call(
        serve_kernel,
        out_shape=[jax.ShapeDtypeStruct((NC * NZ * SLICE, PADDED), BF16)] * NY,
        in_specs=[SCALARS, SCALARS, OUTSIDE, OUTSIDE],
        out_specs=[WHOLE] * NY,
        scratch_shapes=[pltpu.VMEM(pool.shape, BF16), pltpu.SemaphoreType.DMA((1,))],
        compiler_params=pltpu.CompilerParams(vmem_limit_bytes=8 * MIB),
        name="serve",
    )(place, wanted, pool, after)


def sort_kernel(*refs):
    served, (mine_ref, give_ref) = refs[:NY], refs[NY:]
    size = NZ * SLICE
    for by, ref in enumerate(served):
        mine_ref[pl.ds(by * size, size), :] = ref[:size, :]
        give_ref[pl.ds(by * size, size), :] = ref[size:, :]


def sort(served):
    return pl.pallas_call(
        sort_kernel,
        out_shape=[jax.ShapeDtypeStruct((NY * NZ * SLICE, PADDED), BF16)] * 2,
        in_specs=[WHOLE] * NY,
        out_specs=[WHOLE] * 2,
        compiler_params=pltpu.CompilerParams(vmem_limit_bytes=8 * MIB),
        name="sort",
    )(*served)


def pick_kernel(place_ref, owner_ref, mine_ref, theirs_ref, out_ref):
    y, core = place_ref[0], place_ref[2]

    def one(index, carry):
        owner = owner_ref[index]
        line = (y + NY - (owner >> 4)) & (NY - 1)
        row = pl.multiple_of((line * NZ + ((owner >> 1) & (NZ - 1))) * SLICE, SLICE)
        target = pl.ds(pl.multiple_of(index * SLICE, SLICE), SLICE)
        here = (owner & 1) == core

        @pl.when(here)
        def _():
            out_ref[target, :] = mine_ref[pl.ds(row, SLICE), :]

        @pl.when(jnp.logical_not(here))
        def _():
            out_ref[target, :] = theirs_ref[pl.ds(row, SLICE), :]

        return carry

    lax.fori_loop(0, HMAX, one, 0)


def pick(place, owner, mine, theirs):
    return pl.pallas_call(
        pick_kernel,
        out_shape=jax.ShapeDtypeStruct((HMAX * SLICE, PADDED), BF16),
        in_specs=[SCALARS, SCALARS, WHOLE, WHOLE],
        out_specs=WHOLE,
        compiler_params=pltpu.CompilerParams(vmem_limit_bytes=8 * MIB),
        name="pick",
    )(place, owner, mine, theirs)


def norm_kernel(parts_ref, q_gain_ref, kv_gain_ref, cos_ref, sin_ref, after_ref, out_ref, row_ref):
    groups = NY * NC
    wide = COLS // groups
    for group in range(groups):
        total = parts_ref[group * NX]
        for other in range(1, NX):
            total = total + parts_ref[group * NX + other]
        row_ref[:, group * wide : (group + 1) * wide] = total
    query = row_ref[:, :QL]
    scale = lax.rsqrt(jnp.mean(query * query, axis=1, keepdims=True) + EPS)
    out_ref[:, :QL] = (query * scale * q_gain_ref[...]).astype(BF16)
    key = row_ref[:, QL : QL + KL]
    scale = lax.rsqrt(jnp.mean(key * key, axis=1, keepdims=True) + EPS)
    out_ref[:, QL : QL + KL] = (key * scale * kv_gain_ref[...]).astype(BF16)
    rope = rotate(row_ref[:, QL + KL :], cos_ref[...], sin_ref[...])
    out_ref[:, QL + KL :] = rope.astype(BF16)


def norm(parts, q_gain, kv_gain, cosine, sine, after):
    return pl.pallas_call(
        norm_kernel,
        out_shape=jax.ShapeDtypeStruct((QUART, COLS), BF16),
        in_specs=[WHOLE] * 5 + [OUTSIDE],
        out_specs=WHOLE,
        scratch_shapes=[pltpu.VMEM((QUART, COLS), F32)],
        compiler_params=pltpu.CompilerParams(vmem_limit_bytes=8 * MIB),
        name="norm",
    )(parts, q_gain, kv_gain, cosine, sine, after)


def query_kernel(norm_ref, w_ref, up_ref, cos_ref, sin_ref, after_ref, out_ref):
    query = jnp.dot(norm_ref[...], w_ref[...], preferred_element_type=F32).astype(BF16)
    for pair in range(2):
        base = pair * (ND + RD)
        lifted = jnp.dot(
            query[:, base : base + ND], up_ref[pair], preferred_element_type=F32
        )
        out_ref[pair, :, :KL] = lifted.astype(BF16)
        rope = query[:, base + ND : base + ND + RD].astype(F32)
        out_ref[pair, :, KL:WIDTH] = rotate(rope, cos_ref[...], sin_ref[...]).astype(BF16)
        lane = lax.broadcasted_iota(jnp.int32, (out_ref.shape[1], PADDED - WIDTH), 1)
        out_ref[pair, :, WIDTH:] = jnp.where(lane == 0, 1.0, 0.0).astype(BF16)


def queries(q_norm, w_qb, w_uk, cosine, sine, after):
    heads = w_uk.shape[0]
    rows = q_norm.shape[0]
    wide = 2 * (ND + RD)
    return pl.pallas_call(
        query_kernel,
        out_shape=jax.ShapeDtypeStruct((heads, rows, PADDED), BF16),
        grid=(heads // 2,),
        in_specs=[
            pl.BlockSpec((rows, QL), lambda i: (0, 0)),
            pl.BlockSpec((QL, wide), lambda i: (0, i)),
            pl.BlockSpec((2, ND, KL), lambda i: (i, 0, 0)),
            pl.BlockSpec((rows, RD), lambda i: (0, 0)),
            pl.BlockSpec((rows, RD), lambda i: (0, 0)),
            pl.BlockSpec(memory_space=pl.ANY),
        ],
        out_specs=pl.BlockSpec((2, rows, PADDED), lambda i: (i, 0, 0)),
        compiler_params=pltpu.CompilerParams(vmem_limit_bytes=GRANT),
        cost_estimate=pl.CostEstimate(
            flops=2 * rows * QL * QL, bytes_accessed=7 * MIB, transcendentals=0
        ),
        name="queries",
    )(q_norm, w_qb, w_uk, cosine, sine, after)


def move(pairs, sems):
    copies = [
        pltpu.make_async_copy(source, target, sems.at[index])
        for index, (source, target) in enumerate(pairs)
    ]
    for copy in copies:
        copy.start()
    for copy in copies:
        copy.wait()


def stack_kernel(*refs):
    out_ref = refs[-1]
    start = 0
    for ref in refs[:-1]:
        out_ref[pl.ds(start, ref.shape[0]), :] = ref[...]
        start += ref.shape[0]


def stack(*blocks):
    shape = (sum(b.shape[0] for b in blocks), blocks[0].shape[1])
    return pl.pallas_call(
        stack_kernel,
        out_shape=jax.ShapeDtypeStruct(shape, blocks[0].dtype),
        in_specs=[WHOLE] * len(blocks),
        out_specs=WHOLE,
        compiler_params=pltpu.CompilerParams(vmem_limit_bytes=16 * MIB),
        name="stack",
    )(*blocks)


def gate_kernel(*refs):
    del refs


def gate(blocks, *after):
    return pl.pallas_call(
        gate_kernel,
        out_shape=[jax.ShapeDtypeStruct(b.shape, b.dtype) for b in blocks],
        in_specs=[OUTSIDE] * (len(blocks) + len(after)),
        out_specs=[OUTSIDE] * len(blocks),
        input_output_aliases={i: i for i in range(len(blocks))},
        compiler_params=pltpu.CompilerParams(vmem_limit_bytes=4 * MIB),
        name="gate",
    )(*blocks, *after)


def project_kernel(place_ref, down_in, *refs):
    count = NY * NC
    blocks, (out_ref, token_ref, down_ref, sems) = refs[:count], refs[count:]
    pairs = [(down_in, down_ref)] + [(ref, token_ref.at[i]) for i, ref in enumerate(blocks)]
    copies = [
        pltpu.make_async_copy(source, target, sems.at[index])
        for index, (source, target) in enumerate(pairs)
    ]
    for copy in copies:
        copy.start()
    y, core = place_ref[0], place_ref[2]
    copies[0].wait()
    for index in range(count):
        copies[index + 1].wait()
        line = (y + NY - index // NC) & (NY - 1)
        side = core if index % NC == 0 else 1 - core
        out_ref[line, side] = jnp.dot(
            token_ref[index], down_ref[...], preferred_element_type=F32
        )


def project(place, blocks, down):
    rows = blocks[0].shape[0]
    return pl.pallas_call(
        project_kernel,
        out_shape=jax.ShapeDtypeStruct((NY, NC, rows, down.shape[1]), F32),
        in_specs=[SCALARS] + [OUTSIDE] * (len(blocks) + 1),
        out_specs=WHOLE,
        scratch_shapes=[
            pltpu.VMEM((len(blocks),) + blocks[0].shape, BF16),
            pltpu.VMEM(down.shape, BF16),
            pltpu.SemaphoreType.DMA((len(blocks) + 1,)),
        ],
        compiler_params=pltpu.CompilerParams(vmem_limit_bytes=GRANT),
        name="project",
    )(place, down, *blocks)


def spread_kernel(place_ref, normed_ref, after_ref, send_ref):
    x = place_ref[3]
    send_ref[:, WIDTH:] = jnp.zeros((send_ref.shape[0], PADDED - WIDTH), BF16)
    send_ref[:HALF, :WIDTH] = normed_ref[:HALF, QL:]
    first = pl.multiple_of(HALF + x * SIXTEENTH, SIXTEENTH)
    send_ref[HALF:, :WIDTH] = normed_ref[pl.ds(first, SIXTEENTH), QL:]


def spread(place, normed, after):
    return pl.pallas_call(
        spread_kernel,
        out_shape=jax.ShapeDtypeStruct((HALF + SIXTEENTH, PADDED), BF16),
        in_specs=[SCALARS, WHOLE, OUTSIDE],
        out_specs=WHOLE,
        compiler_params=pltpu.CompilerParams(vmem_limit_bytes=8 * MIB),
        name="spread",
    )(place, normed, after)


def split_kernel(line_ref, whole_ref, piece_ref):
    both = HALF + SIXTEENTH
    for index in range(NZ):
        start = index * both
        whole_ref[pl.ds(index * HALF, HALF), :] = line_ref[pl.ds(start, HALF), :]
        piece_ref[pl.ds(index * SIXTEENTH, SIXTEENTH), :] = line_ref[
            pl.ds(start + HALF, SIXTEENTH), :
        ]


def split(line):
    return pl.pallas_call(
        split_kernel,
        out_shape=[
            jax.ShapeDtypeStruct((NZ * HALF, PADDED), BF16),
            jax.ShapeDtypeStruct((NZ * SIXTEENTH, PADDED), BF16),
        ],
        in_specs=[WHOLE],
        out_specs=[WHOLE] * 2,
        compiler_params=pltpu.CompilerParams(vmem_limit_bytes=8 * MIB),
        name="split",
    )(line)


def hide(key_ref, first, size, hidden):
    lane = lax.broadcasted_iota(jnp.int32, (size, PADDED - WIDTH), 1)
    value = jnp.where((lane == 0) & hidden, NEGATIVE, 0.0)
    key_ref[pl.ds(first, size), WIDTH:] = value.astype(BF16)


def fold(state, query_at, key_ref, rows, first, masks):
    top_ref, sum_ref, acc_ref = state

    def score(start):
        return lax.dot_general(
            query_at(start), key_ref[...], (((1,), (1,)), ((), ())), preferred_element_type=F32
        )

    ready = score(0)
    for start in range(0, rows, GROUP):
        scores = ready
        if start + GROUP < rows:
            ready = score(start + GROUP)
        if masks:
            pieces, done = [], 0
            for begin, end, seen in masks:
                if begin > done:
                    pieces.append(scores[:, done:begin])
                pieces.append(jnp.where(seen, scores[:, begin:end], NEGATIVE))
                done = end
            if done < scores.shape[1]:
                pieces.append(scores[:, done:])
            scores = jnp.concatenate(pieces, axis=1)
        part = pl.ds(pl.multiple_of(first + start, GROUP), GROUP)
        before = top_ref[part, :]
        top = jnp.maximum(before, jnp.max(scores, axis=1, keepdims=True))
        weights = jnp.exp2((scores - top) * LOG2)
        shrink = jnp.exp2((before - top) * LOG2)
        top_ref[part, :] = top
        sum_ref[part, :] = sum_ref[part, :] * shrink + jnp.sum(weights, axis=1, keepdims=True)
        acc_ref[part, :] = acc_ref[part, :] * shrink + jnp.dot(
            weights.astype(BF16), key_ref[:, :KL], preferred_element_type=F32
        )


def lift(side, w_ref, out_ref, top_ref, sum_ref, acc_ref):
    heads = w_ref.shape[0]
    for head in range(heads):
        part = pl.ds((side * heads + head) * CH, CH)
        mixed = acc_ref[part, :]
        high = mixed.astype(BF16)
        low = (mixed - high.astype(F32)).astype(BF16)
        weight = w_ref[head]
        lifted = jnp.dot(high, weight, preferred_element_type=F32)
        lifted = lifted + jnp.dot(low, weight, preferred_element_type=F32)
        out_ref[:, head * VD : (head + 1) * VD] = lifted
        at = heads * VD + head
        out_ref[:, at : at + 1] = top_ref[part, :]
        out_ref[:, at + heads : at + heads + 1] = sum_ref[part, :]


def prefix_kernel(place_ref, q_ref, key_in, w_ref, after_ref, out_ref, *scratch):
    top_ref, sum_ref, acc_ref, key_ref, sems = scratch
    state = (top_ref, sum_ref, acc_ref)
    rows = q_ref.shape[0]
    top_ref[...] = jnp.full(top_ref.shape, NEGATIVE, F32)
    sum_ref[...] = jnp.zeros(sum_ref.shape, F32)
    acc_ref[...] = jnp.zeros(acc_ref.shape, F32)
    size = key_ref.shape[0] // NX
    move([(key_in, key_ref)], sems)
    for index in range(NX):
        for slot in range(HMAX):
            if slot >= LEAST:
                hide(key_ref, index * size + slot * SLICE, SLICE, slot >= place_ref[4])
    query_at = lambda start: q_ref[start : start + GROUP, :]
    fold(state, query_at, key_ref, rows, 0, ())
    lift(0, w_ref, out_ref, top_ref, sum_ref, acc_ref)


def state_scratch(rows):
    return [
        pltpu.VMEM((rows, 1), F32),
        pltpu.VMEM((rows, 1), F32),
        pltpu.VMEM((rows, KL), F32),
    ]


def lifted_shape(w_uv):
    return jax.ShapeDtypeStruct((CH, w_uv.shape[0] * VD + CH), F32)


def prefix_pass(place, query, keys, w_uv, after):
    rows = query.shape[0]
    return pl.pallas_call(
        prefix_kernel,
        out_shape=lifted_shape(w_uv),
        in_specs=[SCALARS, WHOLE, OUTSIDE, WHOLE, OUTSIDE],
        out_specs=WHOLE,
        scratch_shapes=state_scratch(rows)
        + [
            pltpu.VMEM(keys.shape, BF16),
            pltpu.SemaphoreType.DMA((1,)),
        ],
        compiler_params=pltpu.CompilerParams(vmem_limit_bytes=GRANT),
        cost_estimate=pl.CostEstimate(
            flops=2 * rows * keys.shape[0] * (WIDTH + KL),
            bytes_accessed=8 * MIB,
            transcendentals=rows * keys.shape[0],
        ),
        name="prefix",
    )(place, query, keys, w_uv, after)


def stretch_kernel(kinds, place_ref, q_ref, *refs):
    pieces, refs = refs[: len(kinds)], refs[len(kinds) :]
    w_ref, _, keep_ref, give_ref, top_ref, sum_ref, acc_ref, key_ref, sems = refs
    copies = []
    for index, ((kind, by), ref) in enumerate(zip(kinds, pieces)):
        if kind == "line" and by:
            line = (place_ref[0] + NY - by) & (NY - 1)
            ref = ref.at[pl.ds(pl.multiple_of(line * PIECE, PIECE), PIECE), :]
        target = key_ref.at[pl.ds(index * PIECE, PIECE), :]
        copies.append(pltpu.make_async_copy(ref, target, sems.at[index]))
        copies[-1].start()
    top_ref[...] = jnp.full(top_ref.shape, NEGATIVE, F32)
    sum_ref[...] = jnp.zeros(sum_ref.shape, F32)
    acc_ref[...] = jnp.zeros(acc_ref.shape, F32)
    y, z, core, x = (place_ref[i] for i in range(4))
    span = (y * NZ + z) * NC + core
    for copy in copies:
        copy.wait()
    mixed = []
    for index, (kind, by) in enumerate(kinds):
        start = index * PIECE
        if kind == "line" and by:
            hide(key_ref, start, PIECE, by > y)
        elif kind == "line":
            lane = lax.broadcasted_iota(jnp.int32, (1, PIECE), 1)
            mixed.append((start, start + PIECE, lane // HALF, lane % HALF))
        else:
            size = NZ * SIXTEENTH
            for line in range(1, NY):
                hide(key_ref, start + line * size, size, line > y)
            lane = lax.broadcasted_iota(jnp.int32, (1, size), 1)
            token = HALF + SIXTEENTH * ((x + NX - by) & (NX - 1)) + lane % SIXTEENTH
            mixed.append((start, start + size, lane // SIXTEENTH, token))
    rows = q_ref.shape[0] // 2

    def side_pass(side, carry):
        base = (span + side * (1 - 2 * core)) * CH
        own = lax.broadcasted_iota(jnp.int32, (GROUP, 1), 0) % CH + base
        masks = [
            (begin, end, ((y * NZ + column) * NC + core) * CH + token <= own)
            for begin, end, column, token in mixed
        ]

        def query_at(start):
            return q_ref[pl.ds(pl.multiple_of(side * rows + start, GROUP), GROUP), :]

        fold((top_ref, sum_ref, acc_ref), query_at, key_ref, rows, side * rows, masks)
        return carry

    lax.fori_loop(0, NC, side_pass, 0)
    lift(0, w_ref, keep_ref, top_ref, sum_ref, acc_ref)
    lift(1, w_ref, give_ref, top_ref, sum_ref, acc_ref)


def stretch_pass(place, query, pieces, w_uv, after):
    rows = query.shape[0]
    kinds = tuple(piece[:2] for piece in pieces)
    arrays = [piece[2] for piece in pieces]
    keys = len(kinds) * PIECE
    operands = [place, query, *arrays, w_uv, after]
    return pl.pallas_call(
        functools.partial(stretch_kernel, kinds),
        out_shape=[lifted_shape(w_uv)] * 2,
        in_specs=[SCALARS, WHOLE] + [OUTSIDE] * len(kinds) + [WHOLE, OUTSIDE],
        out_specs=[WHOLE] * 2,
        scratch_shapes=state_scratch(rows)
        + [
            pltpu.VMEM((keys, PADDED), BF16),
            pltpu.SemaphoreType.DMA((len(kinds),)),
        ],
        compiler_params=pltpu.CompilerParams(vmem_limit_bytes=GRANT),
        cost_estimate=pl.CostEstimate(
            flops=2 * rows * keys * (WIDTH + KL),
            bytes_accessed=8 * MIB,
            transcendentals=rows * keys,
        ),
        name="stretch",
    )(*operands)


def merge_kernel(*refs):
    parts, out_ref = refs[:-1], refs[-1]
    heads = out_ref.shape[1] // VD
    for head in range(heads):
        at = heads * VD + head
        tops = [ref[:, at : at + 1] for ref in parts]
        top = functools.reduce(jnp.maximum, tops)
        total = mixed = 0.0
        for ref, own in zip(parts, tops):
            scale = jnp.exp2((own - top) * LOG2)
            total = total + ref[:, at + heads : at + heads + 1] * scale
            mixed = mixed + ref[:, head * VD : (head + 1) * VD] * scale
        out_ref[:, head * VD : (head + 1) * VD] = (mixed / total).astype(BF16)


def merge(parts):
    return pl.pallas_call(
        merge_kernel,
        out_shape=jax.ShapeDtypeStruct((CH, parts[0].shape[1] - CH), BF16),
        in_specs=[WHOLE] * len(parts),
        out_specs=WHOLE,
        compiler_params=pltpu.CompilerParams(vmem_limit_bytes=12 * MIB),
        name="merge",
    )(*parts)


def body(
    hidden_in,
    w_down,
    q_gain,
    kv_gain,
    w_qb,
    w_uk,
    w_uv,
    cache_pool,
    hit_owner,
    hit_block,
    hit_count,
):
    y = lax.axis_index("y").astype(jnp.int32)
    z = lax.axis_index("z").astype(jnp.int32)
    c = lax.axis_index("c").astype(jnp.int32)
    x = lax.axis_index("x").astype(jnp.int32)
    span = (y * NZ + z) * NC + c
    my_owner = lax.dynamic_index_in_dim(hit_owner, span, 0, keepdims=False)
    my_count = lax.dynamic_index_in_dim(hit_count, span, 0, keepdims=False)
    place = jnp.stack([y, z, c, x, my_count])
    rows = hidden_in.shape[0]
    heads = w_uk.shape[0]
    feats = hidden_in.shape[1]
    parts = NY * NC
    per = w_down.shape[0]
    wide = COLS // parts
    cosine, sine = rope_tables(span * CH + jnp.arange(rows, dtype=jnp.int32))
    quarter = lambda table: lax.dynamic_slice_in_dim(table, x * QUART, QUART, 0)

    pair = NC * per
    hidden = hidden_in.reshape(rows, NY, NZ, pair).transpose(0, 2, 1, 3).reshape(rows, feats)
    pieces = w_down.reshape(per, parts, wide).transpose(1, 0, 2)
    pieces = lax.all_to_all(pieces, ("y", "c"), 0, 0, tiled=True).reshape(parts * per, wide)
    down = lax.all_gather(pieces, "z", axis=0, tiled=True)
    (hidden,) = gate([hidden], pieces, cosine, sine)
    others = gate(offsets(hidden, "y", NY)[1:], down)
    tokens = []
    for block in [hidden, *others]:
        tokens += [block, shift(block, "c", NC, 1)]

    pool = lax.all_gather(quarter_pool(x, cache_pool), "z", axis=0, tiled=True)
    table = lambda array: lax.dynamic_index_in_dim(
        array.reshape(NY, NZ, NC, -1), z, 1, keepdims=False
    )
    live = jnp.arange(HMAX, dtype=jnp.int32) < table(hit_count)
    owners = (y * NZ + jnp.arange(NZ, dtype=jnp.int32)) * NC + c
    asking = (table(hit_owner) == owners[:, None, None, None]) & live
    wanted = jnp.sum(jnp.where(asking, table(hit_block), 0), axis=3)
    wanted = wanted + PB * jnp.arange(NZ, dtype=jnp.int32)[:, None, None]
    wanted = jnp.transpose(wanted, (1, 2, 0)).reshape(-1)
    partial_proj = project(place, tokens, down).reshape(parts * rows, wide)
    arrived = lax.all_to_all(partial_proj, ("y", "c", "x"), 0, 0, tiled=True)
    served = serve(place, wanted, pool, arrived)
    served = [served[0]] + [shift(served[by], "y", NY, by) for by in range(1, NY)]

    normed = norm(
        arrived.reshape(parts * NX, QUART, wide),
        q_gain[None, :],
        kv_gain[None, :],
        quarter(cosine),
        quarter(sine),
        served[0],
    )
    normed = lax.all_gather(normed, "x", axis=0, tiled=True)
    ours, give = sort(served)
    send = spread(place, normed, ours)

    whole, piece = split(lax.all_gather(send, "z", axis=0, tiled=True))
    piece = stack(*offsets(piece, "y", NY))
    lines = lax.all_gather(whole, "y", axis=0, tiled=True)
    planes = offsets(piece, "x", NX)
    prefix = pick(place, my_owner, ours, shift(give, "c", NC, 1))
    prefix_all = lax.all_gather(prefix, "x", axis=0, tiled=True)

    query = queries(normed, w_qb, w_uk, cosine, sine, piece).reshape(heads * rows, PADDED)
    query_all = stack(query, shift(query, "c", NC, 1))

    parts = []
    for pieces in (
        [("line", 0, whole), ("plane", 0, planes[0])],
        [("line", 1, lines), ("line", 2, lines), ("line", 3, lines), ("plane", 1, planes[1])],
        [("plane", 3, planes[3]), ("plane", 2, planes[2])],
    ):
        keep, give = stretch_pass(place, query_all, pieces, w_uv, parts[-2] if parts else piece)
        parts += [keep, shift(give, "c", NC, 1)]
    parts.append(prefix_pass(place, query, prefix_all, w_uv, parts[-2]))
    return merge(parts)


def solution(mesh):
    fine = Mesh(mesh.devices.reshape(NY, NZ, NC, NX), ("y", "z", "c", "x"))
    span = SPAN_AXES
    in_specs = (
        P(span, "x"),
        P(("x",) + span, None),
        P(),
        P(),
        P(None, "x"),
        P("x", None, None),
        P("x", None, None),
        P(span, None, None),
        P(),
        P(),
        P(),
    )
    return jax.shard_map(
        body, mesh=fine, in_specs=in_specs, out_specs=P(span, "x"), check_vma=False
    )
```

```python
import functools
import math

import jax
import jax.numpy as jnp
from jax import lax
from jax.experimental import pallas as pl
from jax.experimental.pallas import tpu as pltpu
from jax.sharding import Mesh, PartitionSpec as P

QL = 1536
KL = 512
RD = 64
ND = 128
VD = 128
WIDTH = KL + RD
PADDED = 640
COLS = QL + KL + RD
CH = 128
BLK = 64
PB = 8
HMAX = 27
LEAST = 25
NY, NZ, NC, NX = 4, 8, 2, 4
QUART = CH // NX
HALF = CH // 2
SIXTEENTH = HALF // NX
PIECE = NZ * HALF
SLICE = BLK // NX
GROUP = 256
SPAN_AXES = ("y", "z", "c")

ROPE_BASE = 50000.0
EPS = 1e-06
NEGATIVE = -1e30
LOG2 = math.log2(math.e) / math.sqrt(ND + RD)
F32 = jnp.float32
BF16 = jnp.bfloat16
MIB = 1 << 20
GRANT = 56 * MIB
WHOLE = pl.BlockSpec(memory_space=pltpu.VMEM)
SCALARS = pl.BlockSpec(memory_space=pltpu.SMEM)
OUTSIDE = pl.BlockSpec(memory_space=pl.ANY)


def shift(value, axis, size, by):
    return lax.ppermute(value, axis, [(i, (i + by) % size) for i in range(size)])


def offsets(block, axis, size):
    return [block] + [shift(block, axis, size, by) for by in range(1, size)]


def rope_tables(positions):
    half = RD // 2
    freqs = ROPE_BASE ** (-jnp.arange(half, dtype=F32) / half)
    angles = positions.astype(F32)[:, None] * freqs[None, :]
    cosine = jnp.cos(angles)
    sine = jnp.sin(angles)
    return (
        jnp.concatenate([cosine, cosine], axis=1),
        jnp.concatenate([-sine, sine], axis=1),
    )


def rotate(vec, cosine, sine):
    half = RD // 2
    swapped = jnp.concatenate([vec[:, half:], vec[:, :half]], axis=1)
    return vec * cosine + swapped * sine


def quarter_kernel(x_ref, pool_ref, out_ref):
    first = pl.multiple_of(x_ref[0] * SLICE, SLICE)
    for index in range(pool_ref.shape[0]):
        part = pl.ds(index * SLICE, SLICE)
        out_ref[part, :WIDTH] = pool_ref[index, pl.ds(first, SLICE), :]
        out_ref[part, WIDTH:] = jnp.zeros((SLICE, PADDED - WIDTH), BF16)


def quarter_pool(x, pool):
    return pl.pallas_call(
        quarter_kernel,
        out_shape=jax.ShapeDtypeStruct((pool.shape[0] * SLICE, PADDED), BF16),
        in_specs=[SCALARS, WHOLE],
        out_specs=WHOLE,
        compiler_params=pltpu.CompilerParams(vmem_limit_bytes=8 * MIB),
        name="quarter",
    )(x.reshape(1), pool)


def serve_kernel(place_ref, wanted_ref, pool_in, after_ref, *refs):
    out_refs, (pool_ref, sems) = refs[:NY], refs[NY:]
    move([(pool_in, pool_ref)], sems)
    y, core = place_ref[0], place_ref[2]
    for by, out_ref in enumerate(out_refs):
        line = (y + by) & (NY - 1)
        for other in range(NC):
            side = core if other == 0 else 1 - core
            for index in range(NZ):
                block = wanted_ref[(line * NC + side) * NZ + index]
                row = pl.multiple_of(block * SLICE, SLICE)
                start = (other * NZ + index) * SLICE
                out_ref[pl.ds(start, SLICE), :] = pool_ref[pl.ds(row, SLICE), :]


def serve(place, wanted, pool, after):
    return pl.pallas_call(
        serve_kernel,
        out_shape=[jax.ShapeDtypeStruct((NC * NZ * SLICE, PADDED), BF16)] * NY,
        in_specs=[SCALARS, SCALARS, OUTSIDE, OUTSIDE],
        out_specs=[WHOLE] * NY,
        scratch_shapes=[pltpu.VMEM(pool.shape, BF16), pltpu.SemaphoreType.DMA((1,))],
        compiler_params=pltpu.CompilerParams(vmem_limit_bytes=8 * MIB),
        name="serve",
    )(place, wanted, pool, after)


def sort_kernel(*refs):
    served, (mine_ref, give_ref) = refs[:NY], refs[NY:]
    size = NZ * SLICE
    for by, ref in enumerate(served):
        mine_ref[pl.ds(by * size, size), :] = ref[:size, :]
        give_ref[pl.ds(by * size, size), :] = ref[size:, :]


def sort(served):
    return pl.pallas_call(
        sort_kernel,
        out_shape=[jax.ShapeDtypeStruct((NY * NZ * SLICE, PADDED), BF16)] * 2,
        in_specs=[WHOLE] * NY,
        out_specs=[WHOLE] * 2,
        compiler_params=pltpu.CompilerParams(vmem_limit_bytes=8 * MIB),
        name="sort",
    )(*served)


def pick_kernel(place_ref, owner_ref, mine_ref, theirs_ref, out_ref):
    y, core = place_ref[0], place_ref[2]

    def one(index, carry):
        owner = owner_ref[index]
        line = (y + NY - (owner >> 4)) & (NY - 1)
        row = pl.multiple_of((line * NZ + ((owner >> 1) & (NZ - 1))) * SLICE, SLICE)
        target = pl.ds(pl.multiple_of(index * SLICE, SLICE), SLICE)
        here = (owner & 1) == core

        @pl.when(here)
        def _():
            out_ref[target, :] = mine_ref[pl.ds(row, SLICE), :]

        @pl.when(jnp.logical_not(here))
        def _():
            out_ref[target, :] = theirs_ref[pl.ds(row, SLICE), :]

        return carry

    lax.fori_loop(0, HMAX, one, 0)


def pick(place, owner, mine, theirs):
    return pl.pallas_call(
        pick_kernel,
        out_shape=jax.ShapeDtypeStruct((HMAX * SLICE, PADDED), BF16),
        in_specs=[SCALARS, SCALARS, WHOLE, WHOLE],
        out_specs=WHOLE,
        compiler_params=pltpu.CompilerParams(vmem_limit_bytes=8 * MIB),
        name="pick",
    )(place, owner, mine, theirs)


def norm_kernel(parts_ref, q_gain_ref, kv_gain_ref, cos_ref, sin_ref, after_ref, out_ref, row_ref):
    groups = NY * NC
    wide = COLS // groups
    for group in range(groups):
        total = parts_ref[group * NX]
        for other in range(1, NX):
            total = total + parts_ref[group * NX + other]
        row_ref[:, group * wide : (group + 1) * wide] = total
    query = row_ref[:, :QL]
    scale = lax.rsqrt(jnp.mean(query * query, axis=1, keepdims=True) + EPS)
    out_ref[:, :QL] = (query * scale * q_gain_ref[...]).astype(BF16)
    key = row_ref[:, QL : QL + KL]
    scale = lax.rsqrt(jnp.mean(key * key, axis=1, keepdims=True) + EPS)
    out_ref[:, QL : QL + KL] = (key * scale * kv_gain_ref[...]).astype(BF16)
    rope = rotate(row_ref[:, QL + KL :], cos_ref[...], sin_ref[...])
    out_ref[:, QL + KL :] = rope.astype(BF16)


def norm(parts, q_gain, kv_gain, cosine, sine, after):
    return pl.pallas_call(
        norm_kernel,
        out_shape=jax.ShapeDtypeStruct((QUART, COLS), BF16),
        in_specs=[WHOLE] * 5 + [OUTSIDE],
        out_specs=WHOLE,
        scratch_shapes=[pltpu.VMEM((QUART, COLS), F32)],
        compiler_params=pltpu.CompilerParams(vmem_limit_bytes=8 * MIB),
        name="norm",
    )(parts, q_gain, kv_gain, cosine, sine, after)


def query_kernel(norm_ref, w_ref, up_ref, cos_ref, sin_ref, after_ref, out_ref):
    query = jnp.dot(norm_ref[...], w_ref[...], preferred_element_type=F32).astype(BF16)
    for pair in range(2):
        base = pair * (ND + RD)
        lifted = jnp.dot(
            query[:, base : base + ND], up_ref[pair], preferred_element_type=F32
        )
        out_ref[pair, :, :KL] = lifted.astype(BF16)
        rope = query[:, base + ND : base + ND + RD].astype(F32)
        out_ref[pair, :, KL:WIDTH] = rotate(rope, cos_ref[...], sin_ref[...]).astype(BF16)
        lane = lax.broadcasted_iota(jnp.int32, (out_ref.shape[1], PADDED - WIDTH), 1)
        out_ref[pair, :, WIDTH:] = jnp.where(lane == 0, 1.0, 0.0).astype(BF16)


def queries(q_norm, w_qb, w_uk, cosine, sine, after):
    heads = w_uk.shape[0]
    rows = q_norm.shape[0]
    wide = 2 * (ND + RD)
    return pl.pallas_call(
        query_kernel,
        out_shape=jax.ShapeDtypeStruct((heads, rows, PADDED), BF16),
        grid=(heads // 2,),
        in_specs=[
            pl.BlockSpec((rows, QL), lambda i: (0, 0)),
            pl.BlockSpec((QL, wide), lambda i: (0, i)),
            pl.BlockSpec((2, ND, KL), lambda i: (i, 0, 0)),
            pl.BlockSpec((rows, RD), lambda i: (0, 0)),
            pl.BlockSpec((rows, RD), lambda i: (0, 0)),
            pl.BlockSpec(memory_space=pl.ANY),
        ],
        out_specs=pl.BlockSpec((2, rows, PADDED), lambda i: (i, 0, 0)),
        compiler_params=pltpu.CompilerParams(vmem_limit_bytes=GRANT),
        cost_estimate=pl.CostEstimate(
            flops=2 * rows * QL * QL, bytes_accessed=7 * MIB, transcendentals=0
        ),
        name="queries",
    )(q_norm, w_qb, w_uk, cosine, sine, after)


def move(pairs, sems):
    copies = [
        pltpu.make_async_copy(source, target, sems.at[index])
        for index, (source, target) in enumerate(pairs)
    ]
    for copy in copies:
        copy.start()
    for copy in copies:
        copy.wait()


def stack_kernel(*refs):
    out_ref = refs[-1]
    start = 0
    for ref in refs[:-1]:
        out_ref[pl.ds(start, ref.shape[0]), :] = ref[...]
        start += ref.shape[0]


def stack(*blocks):
    shape = (sum(b.shape[0] for b in blocks), blocks[0].shape[1])
    return pl.pallas_call(
        stack_kernel,
        out_shape=jax.ShapeDtypeStruct(shape, blocks[0].dtype),
        in_specs=[WHOLE] * len(blocks),
        out_specs=WHOLE,
        compiler_params=pltpu.CompilerParams(vmem_limit_bytes=16 * MIB),
        name="stack",
    )(*blocks)


def gate_kernel(*refs):
    del refs


def gate(blocks, *after):
    return pl.pallas_call(
        gate_kernel,
        out_shape=[jax.ShapeDtypeStruct(b.shape, b.dtype) for b in blocks],
        in_specs=[OUTSIDE] * (len(blocks) + len(after)),
        out_specs=[OUTSIDE] * len(blocks),
        input_output_aliases={i: i for i in range(len(blocks))},
        compiler_params=pltpu.CompilerParams(vmem_limit_bytes=4 * MIB),
        name="gate",
    )(*blocks, *after)


def project_kernel(place_ref, down_in, *refs):
    count = NY * NC
    blocks, (out_ref, token_ref, down_ref, sems) = refs[:count], refs[count:]
    pairs = [(down_in, down_ref)] + [(ref, token_ref.at[i]) for i, ref in enumerate(blocks)]
    copies = [
        pltpu.make_async_copy(source, target, sems.at[index])
        for index, (source, target) in enumerate(pairs)
    ]
    for copy in copies:
        copy.start()
    y, core = place_ref[0], place_ref[2]
    copies[0].wait()
    for index in range(count):
        copies[index + 1].wait()
        line = (y + NY - index // NC) & (NY - 1)
        side = core if index % NC == 0 else 1 - core
        out_ref[line, side] = jnp.dot(
            token_ref[index], down_ref[...], preferred_element_type=F32
        )


def project(place, blocks, down):
    rows = blocks[0].shape[0]
    return pl.pallas_call(
        project_kernel,
        out_shape=jax.ShapeDtypeStruct((NY, NC, rows, down.shape[1]), F32),
        in_specs=[SCALARS] + [OUTSIDE] * (len(blocks) + 1),
        out_specs=WHOLE,
        scratch_shapes=[
            pltpu.VMEM((len(blocks),) + blocks[0].shape, BF16),
            pltpu.VMEM(down.shape, BF16),
            pltpu.SemaphoreType.DMA((len(blocks) + 1,)),
        ],
        compiler_params=pltpu.CompilerParams(vmem_limit_bytes=GRANT),
        name="project",
    )(place, down, *blocks)


def spread_kernel(place_ref, normed_ref, after_ref, send_ref):
    x = place_ref[3]
    send_ref[:, WIDTH:] = jnp.zeros((send_ref.shape[0], PADDED - WIDTH), BF16)
    send_ref[:HALF, :WIDTH] = normed_ref[:HALF, QL:]
    first = pl.multiple_of(HALF + x * SIXTEENTH, SIXTEENTH)
    send_ref[HALF:, :WIDTH] = normed_ref[pl.ds(first, SIXTEENTH), QL:]


def spread(place, normed, after):
    return pl.pallas_call(
        spread_kernel,
        out_shape=jax.ShapeDtypeStruct((HALF + SIXTEENTH, PADDED), BF16),
        in_specs=[SCALARS, WHOLE, OUTSIDE],
        out_specs=WHOLE,
        compiler_params=pltpu.CompilerParams(vmem_limit_bytes=8 * MIB),
        name="spread",
    )(place, normed, after)


def split_kernel(line_ref, whole_ref, piece_ref):
    both = HALF + SIXTEENTH
    for index in range(NZ):
        start = index * both
        whole_ref[pl.ds(index * HALF, HALF), :] = line_ref[pl.ds(start, HALF), :]
        piece_ref[pl.ds(index * SIXTEENTH, SIXTEENTH), :] = line_ref[
            pl.ds(start + HALF, SIXTEENTH), :
        ]


def split(line):
    return pl.pallas_call(
        split_kernel,
        out_shape=[
            jax.ShapeDtypeStruct((NZ * HALF, PADDED), BF16),
            jax.ShapeDtypeStruct((NZ * SIXTEENTH, PADDED), BF16),
        ],
        in_specs=[WHOLE],
        out_specs=[WHOLE] * 2,
        compiler_params=pltpu.CompilerParams(vmem_limit_bytes=8 * MIB),
        name="split",
    )(line)


def hide(key_ref, first, size, hidden):
    lane = lax.broadcasted_iota(jnp.int32, (size, PADDED - WIDTH), 1)
    value = jnp.where((lane == 0) & hidden, NEGATIVE, 0.0)
    key_ref[pl.ds(first, size), WIDTH:] = value.astype(BF16)


def fold(state, query_at, key_ref, rows, first, masks):
    top_ref, sum_ref, acc_ref = state

    def score(start):
        return lax.dot_general(
            query_at(start), key_ref[...], (((1,), (1,)), ((), ())), preferred_element_type=F32
        )

    ready = score(0)
    for start in range(0, rows, GROUP):
        scores = ready
        if start + GROUP < rows:
            ready = score(start + GROUP)
        if masks:
            pieces, done = [], 0
            for begin, end, seen in masks:
                if begin > done:
                    pieces.append(scores[:, done:begin])
                pieces.append(jnp.where(seen, scores[:, begin:end], NEGATIVE))
                done = end
            if done < scores.shape[1]:
                pieces.append(scores[:, done:])
            scores = jnp.concatenate(pieces, axis=1)
        part = pl.ds(pl.multiple_of(first + start, GROUP), GROUP)
        before = top_ref[part, :]
        top = jnp.maximum(before, jnp.max(scores, axis=1, keepdims=True))
        weights = jnp.exp2((scores - top) * LOG2)
        shrink = jnp.exp2((before - top) * LOG2)
        top_ref[part, :] = top
        sum_ref[part, :] = sum_ref[part, :] * shrink + jnp.sum(weights, axis=1, keepdims=True)
        acc_ref[part, :] = acc_ref[part, :] * shrink + jnp.dot(
            weights.astype(BF16), key_ref[:, :KL], preferred_element_type=F32
        )


def lift(side, w_ref, out_ref, top_ref, sum_ref, acc_ref):
    heads = w_ref.shape[0]
    for head in range(heads):
        part = pl.ds((side * heads + head) * CH, CH)
        mixed = acc_ref[part, :]
        high = mixed.astype(BF16)
        low = (mixed - high.astype(F32)).astype(BF16)
        weight = w_ref[head]
        lifted = jnp.dot(high, weight, preferred_element_type=F32)
        lifted = lifted + jnp.dot(low, weight, preferred_element_type=F32)
        out_ref[:, head * VD : (head + 1) * VD] = lifted
        at = heads * VD + head
        out_ref[:, at : at + 1] = top_ref[part, :]
        out_ref[:, at + heads : at + heads + 1] = sum_ref[part, :]


def prefix_kernel(place_ref, q_ref, key_in, w_ref, after_ref, out_ref, *scratch):
    top_ref, sum_ref, acc_ref, key_ref, sems = scratch
    state = (top_ref, sum_ref, acc_ref)
    rows = q_ref.shape[0]
    top_ref[...] = jnp.full(top_ref.shape, NEGATIVE, F32)
    sum_ref[...] = jnp.zeros(sum_ref.shape, F32)
    acc_ref[...] = jnp.zeros(acc_ref.shape, F32)
    size = key_ref.shape[0] // NX
    move([(key_in, key_ref)], sems)
    for index in range(NX):
        for slot in range(HMAX):
            if slot >= LEAST:
                hide(key_ref, index * size + slot * SLICE, SLICE, slot >= place_ref[4])
    query_at = lambda start: q_ref[start : start + GROUP, :]
    fold(state, query_at, key_ref, rows, 0, ())
    lift(0, w_ref, out_ref, top_ref, sum_ref, acc_ref)


def state_scratch(rows):
    return [
        pltpu.VMEM((rows, 1), F32),
        pltpu.VMEM((rows, 1), F32),
        pltpu.VMEM((rows, KL), F32),
    ]


def lifted_shape(w_uv):
    return jax.ShapeDtypeStruct((CH, w_uv.shape[0] * VD + CH), F32)


def prefix_pass(place, query, keys, w_uv, after):
    rows = query.shape[0]
    return pl.pallas_call(
        prefix_kernel,
        out_shape=lifted_shape(w_uv),
        in_specs=[SCALARS, WHOLE, OUTSIDE, WHOLE, OUTSIDE],
        out_specs=WHOLE,
        scratch_shapes=state_scratch(rows)
        + [
            pltpu.VMEM(keys.shape, BF16),
            pltpu.SemaphoreType.DMA((1,)),
        ],
        compiler_params=pltpu.CompilerParams(vmem_limit_bytes=GRANT),
        cost_estimate=pl.CostEstimate(
            flops=2 * rows * keys.shape[0] * (WIDTH + KL),
            bytes_accessed=8 * MIB,
            transcendentals=rows * keys.shape[0],
        ),
        name="prefix",
    )(place, query, keys, w_uv, after)


def stretch_kernel(kinds, place_ref, q_ref, *refs):
    pieces, refs = refs[: len(kinds)], refs[len(kinds) :]
    w_ref, _, keep_ref, give_ref, top_ref, sum_ref, acc_ref, key_ref, sems = refs
    copies = []
    for index, ((kind, by), ref) in enumerate(zip(kinds, pieces)):
        if kind == "line" and by:
            line = (place_ref[0] + NY - by) & (NY - 1)
            ref = ref.at[pl.ds(pl.multiple_of(line * PIECE, PIECE), PIECE), :]
        target = key_ref.at[pl.ds(index * PIECE, PIECE), :]
        copies.append(pltpu.make_async_copy(ref, target, sems.at[index]))
        copies[-1].start()
    top_ref[...] = jnp.full(top_ref.shape, NEGATIVE, F32)
    sum_ref[...] = jnp.zeros(sum_ref.shape, F32)
    acc_ref[...] = jnp.zeros(acc_ref.shape, F32)
    y, z, core, x = (place_ref[i] for i in range(4))
    span = (y * NZ + z) * NC + core
    for copy in copies:
        copy.wait()
    mixed = []
    for index, (kind, by) in enumerate(kinds):
        start = index * PIECE
        if kind == "line" and by:
            hide(key_ref, start, PIECE, by > y)
        elif kind == "line":
            lane = lax.broadcasted_iota(jnp.int32, (1, PIECE), 1)
            mixed.append((start, start + PIECE, lane // HALF, lane % HALF))
        else:
            size = NZ * SIXTEENTH
            for line in range(1, NY):
                hide(key_ref, start + line * size, size, line > y)
            lane = lax.broadcasted_iota(jnp.int32, (1, size), 1)
            token = HALF + SIXTEENTH * ((x + NX - by) & (NX - 1)) + lane % SIXTEENTH
            mixed.append((start, start + size, lane // SIXTEENTH, token))
    rows = q_ref.shape[0] // 2

    def side_pass(side, carry):
        base = (span + side * (1 - 2 * core)) * CH
        own = lax.broadcasted_iota(jnp.int32, (GROUP, 1), 0) % CH + base
        masks = [
            (begin, end, ((y * NZ + column) * NC + core) * CH + token <= own)
            for begin, end, column, token in mixed
        ]

        def query_at(start):
            return q_ref[pl.ds(pl.multiple_of(side * rows + start, GROUP), GROUP), :]

        fold((top_ref, sum_ref, acc_ref), query_at, key_ref, rows, side * rows, masks)
        return carry

    lax.fori_loop(0, NC, side_pass, 0)
    lift(0, w_ref, keep_ref, top_ref, sum_ref, acc_ref)
    lift(1, w_ref, give_ref, top_ref, sum_ref, acc_ref)


def stretch_pass(place, query, pieces, w_uv, after):
    rows = query.shape[0]
    kinds = tuple(piece[:2] for piece in pieces)
    arrays = [piece[2] for piece in pieces]
    keys = len(kinds) * PIECE
    operands = [place, query, *arrays, w_uv, after]
    return pl.pallas_call(
        functools.partial(stretch_kernel, kinds),
        out_shape=[lifted_shape(w_uv)] * 2,
        in_specs=[SCALARS, WHOLE] + [OUTSIDE] * len(kinds) + [WHOLE, OUTSIDE],
        out_specs=[WHOLE] * 2,
        scratch_shapes=state_scratch(rows)
        + [
            pltpu.VMEM((keys, PADDED), BF16),
            pltpu.SemaphoreType.DMA((len(kinds),)),
        ],
        compiler_params=pltpu.CompilerParams(vmem_limit_bytes=GRANT),
        cost_estimate=pl.CostEstimate(
            flops=2 * rows * keys * (WIDTH + KL),
            bytes_accessed=8 * MIB,
            transcendentals=rows * keys,
        ),
        name="stretch",
    )(*operands)


def merge_kernel(*refs):
    parts, out_ref = refs[:-1], refs[-1]
    heads = out_ref.shape[1] // VD
    for head in range(heads):
        at = heads * VD + head
        tops = [ref[:, at : at + 1] for ref in parts]
        top = functools.reduce(jnp.maximum, tops)
        total = mixed = 0.0
        for ref, own in zip(parts, tops):
            scale = jnp.exp2((own - top) * LOG2)
            total = total + ref[:, at + heads : at + heads + 1] * scale
            mixed = mixed + ref[:, head * VD : (head + 1) * VD] * scale
        out_ref[:, head * VD : (head + 1) * VD] = (mixed / total).astype(BF16)


def merge(parts):
    return pl.pallas_call(
        merge_kernel,
        out_shape=jax.ShapeDtypeStruct((CH, parts[0].shape[1] - CH), BF16),
        in_specs=[WHOLE] * len(parts),
        out_specs=WHOLE,
        compiler_params=pltpu.CompilerParams(vmem_limit_bytes=12 * MIB),
        name="merge",
    )(*parts)


def body(
    hidden_in,
    w_down,
    q_gain,
    kv_gain,
    w_qb,
    w_uk,
    w_uv,
    cache_pool,
    hit_owner,
    hit_block,
    hit_count,
):
    y = lax.axis_index("y").astype(jnp.int32)
    z = lax.axis_index("z").astype(jnp.int32)
    c = lax.axis_index("c").astype(jnp.int32)
    x = lax.axis_index("x").astype(jnp.int32)
    span = (y * NZ + z) * NC + c
    my_owner = lax.dynamic_index_in_dim(hit_owner, span, 0, keepdims=False)
    my_count = lax.dynamic_index_in_dim(hit_count, span, 0, keepdims=False)
    place = jnp.stack([y, z, c, x, my_count])
    rows = hidden_in.shape[0]
    heads = w_uk.shape[0]
    feats = hidden_in.shape[1]
    parts = NY * NC
    per = w_down.shape[0]
    wide = COLS // parts
    cosine, sine = rope_tables(span * CH + jnp.arange(rows, dtype=jnp.int32))
    quarter = lambda table: lax.dynamic_slice_in_dim(table, x * QUART, QUART, 0)

    pair = NC * per
    hidden = hidden_in.reshape(rows, NY, NZ, pair).transpose(0, 2, 1, 3).reshape(rows, feats)
    pieces = w_down.reshape(per, parts, wide).transpose(1, 0, 2)
    pieces = lax.all_to_all(pieces, ("y", "c"), 0, 0, tiled=True).reshape(parts * per, wide)
    down = lax.all_gather(pieces, "z", axis=0, tiled=True)
    (hidden,) = gate([hidden], pieces, cosine, sine)
    others = gate(offsets(hidden, "y", NY)[1:], down)
    tokens = []
    for block in [hidden, *others]:
        tokens += [block, shift(block, "c", NC, 1)]

    pool = lax.all_gather(quarter_pool(x, cache_pool), "z", axis=0, tiled=True)
    table = lambda array: lax.dynamic_index_in_dim(
        array.reshape(NY, NZ, NC, -1), z, 1, keepdims=False
    )
    live = jnp.arange(HMAX, dtype=jnp.int32) < table(hit_count)
    owners = (y * NZ + jnp.arange(NZ, dtype=jnp.int32)) * NC + c
    asking = (table(hit_owner) == owners[:, None, None, None]) & live
    wanted = jnp.sum(jnp.where(asking, table(hit_block), 0), axis=3)
    wanted = wanted + PB * jnp.arange(NZ, dtype=jnp.int32)[:, None, None]
    wanted = jnp.transpose(wanted, (1, 2, 0)).reshape(-1)
    partial_proj = project(place, tokens, down).reshape(parts * rows, wide)
    arrived = lax.all_to_all(partial_proj, ("y", "c", "x"), 0, 0, tiled=True)
    served = serve(place, wanted, pool, arrived)
    served = [served[0]] + [shift(served[by], "y", NY, by) for by in range(1, NY)]

    normed = norm(
        arrived.reshape(parts * NX, QUART, wide),
        q_gain[None, :],
        kv_gain[None, :],
        quarter(cosine),
        quarter(sine),
        served[0],
    )
    normed = lax.all_gather(normed, "x", axis=0, tiled=True)
    ours, give = sort(served)
    send = spread(place, normed, ours)

    whole, piece = split(lax.all_gather(send, "z", axis=0, tiled=True))
    piece = stack(*offsets(piece, "y", NY))
    lines = lax.all_gather(whole, "y", axis=0, tiled=True)
    planes = offsets(piece, "x", NX)
    prefix = pick(place, my_owner, ours, shift(give, "c", NC, 1))
    prefix_all = lax.all_gather(prefix, "x", axis=0, tiled=True)

    query = queries(normed, w_qb, w_uk, cosine, sine, piece).reshape(heads * rows, PADDED)
    query_all = stack(query, shift(query, "c", NC, 1))

    parts = []
    for pieces in (
        [("line", 0, whole), ("plane", 0, planes[0])],
        [("line", by, lines) for by in (1, 2, 3)],
        [("plane", by, planes[by]) for by in (1, 3, 2)],
    ):
        keep, give = stretch_pass(place, query_all, pieces, w_uv, parts[-2] if parts else piece)
        parts += [keep, shift(give, "c", NC, 1)]
    parts.append(prefix_pass(place, query, prefix_all, w_uv, parts[-2]))
    return merge(parts)


def solution(mesh):
    fine = Mesh(mesh.devices.reshape(NY, NZ, NC, NX), ("y", "z", "c", "x"))
    span = SPAN_AXES
    in_specs = (
        P(span, "x"),
        P(("x",) + span, None),
        P(),
        P(),
        P(None, "x"),
        P("x", None, None),
        P("x", None, None),
        P(span, None, None),
        P(),
        P(),
        P(),
    )
    return jax.shard_map(
        body, mesh=fine, in_specs=in_specs, out_specs=P(span, "x"), check_vma=False
    )
```

```python
import functools
import math

import jax
import jax.numpy as jnp
from jax import lax
from jax.experimental import pallas as pl
from jax.experimental.pallas import tpu as pltpu
from jax.sharding import Mesh, PartitionSpec as P

QL = 1536
KL = 512
RD = 64
ND = 128
VD = 128
WIDTH = KL + RD
PADDED = 640
COLS = QL + KL + RD
CH = 128
BLK = 64
PB = 8
HMAX = 27
LEAST = 25
NY, NZ, NC, NX = 4, 8, 2, 4
QUART = CH // NX
HALF = CH // 2
SIXTEENTH = HALF // NX
PIECE = NZ * HALF
SLICE = BLK // NX
GROUP = 256
SPAN_AXES = ("y", "z", "c")

ROPE_BASE = 50000.0
EPS = 1e-06
NEGATIVE = -1e30
LOG2 = math.log2(math.e) / math.sqrt(ND + RD)
F32 = jnp.float32
BF16 = jnp.bfloat16
MIB = 1 << 20
GRANT = 56 * MIB
WHOLE = pl.BlockSpec(memory_space=pltpu.VMEM)
SCALARS = pl.BlockSpec(memory_space=pltpu.SMEM)
OUTSIDE = pl.BlockSpec(memory_space=pl.ANY)


def shift(value, axis, size, by):
    return lax.ppermute(value, axis, [(i, (i + by) % size) for i in range(size)])


def offsets(block, axis, size):
    return [block] + [shift(block, axis, size, by) for by in range(1, size)]


def rope_tables(positions):
    half = RD // 2
    freqs = ROPE_BASE ** (-jnp.arange(half, dtype=F32) / half)
    angles = positions.astype(F32)[:, None] * freqs[None, :]
    cosine = jnp.cos(angles)
    sine = jnp.sin(angles)
    return (
        jnp.concatenate([cosine, cosine], axis=1),
        jnp.concatenate([-sine, sine], axis=1),
    )


def rotate(vec, cosine, sine):
    half = RD // 2
    swapped = jnp.concatenate([vec[:, half:], vec[:, :half]], axis=1)
    return vec * cosine + swapped * sine


def quarter_kernel(x_ref, pool_ref, out_ref):
    first = pl.multiple_of(x_ref[0] * SLICE, SLICE)
    for index in range(pool_ref.shape[0]):
        part = pl.ds(index * SLICE, SLICE)
        out_ref[part, :WIDTH] = pool_ref[index, pl.ds(first, SLICE), :]
        out_ref[part, WIDTH:] = jnp.zeros((SLICE, PADDED - WIDTH), BF16)


def quarter_pool(x, pool):
    return pl.pallas_call(
        quarter_kernel,
        out_shape=jax.ShapeDtypeStruct((pool.shape[0] * SLICE, PADDED), BF16),
        in_specs=[SCALARS, WHOLE],
        out_specs=WHOLE,
        compiler_params=pltpu.CompilerParams(vmem_limit_bytes=8 * MIB),
        name="quarter",
    )(x.reshape(1), pool)


def serve_kernel(place_ref, wanted_ref, pool_in, after_ref, *refs):
    out_refs, (pool_ref, sems) = refs[:NY], refs[NY:]
    move([(pool_in, pool_ref)], sems)
    y, core = place_ref[0], place_ref[2]
    for by, out_ref in enumerate(out_refs):
        line = (y + by) & (NY - 1)
        for other in range(NC):
            side = core if other == 0 else 1 - core
            for index in range(NZ):
                block = wanted_ref[(line * NC + side) * NZ + index]
                row = pl.multiple_of(block * SLICE, SLICE)
                start = (other * NZ + index) * SLICE
                out_ref[pl.ds(start, SLICE), :] = pool_ref[pl.ds(row, SLICE), :]


def serve(place, wanted, pool, after):
    return pl.pallas_call(
        serve_kernel,
        out_shape=[jax.ShapeDtypeStruct((NC * NZ * SLICE, PADDED), BF16)] * NY,
        in_specs=[SCALARS, SCALARS, OUTSIDE, OUTSIDE],
        out_specs=[WHOLE] * NY,
        scratch_shapes=[pltpu.VMEM(pool.shape, BF16), pltpu.SemaphoreType.DMA((1,))],
        compiler_params=pltpu.CompilerParams(vmem_limit_bytes=8 * MIB),
        name="serve",
    )(place, wanted, pool, after)


def sort_kernel(*refs):
    served, (mine_ref, give_ref) = refs[:NY], refs[NY:]
    size = NZ * SLICE
    for by, ref in enumerate(served):
        mine_ref[pl.ds(by * size, size), :] = ref[:size, :]
        give_ref[pl.ds(by * size, size), :] = ref[size:, :]


def sort(served):
    return pl.pallas_call(
        sort_kernel,
        out_shape=[jax.ShapeDtypeStruct((NY * NZ * SLICE, PADDED), BF16)] * 2,
        in_specs=[WHOLE] * NY,
        out_specs=[WHOLE] * 2,
        compiler_params=pltpu.CompilerParams(vmem_limit_bytes=8 * MIB),
        name="sort",
    )(*served)


def pick_kernel(place_ref, owner_ref, mine_ref, theirs_ref, out_ref):
    y, core = place_ref[0], place_ref[2]

    def one(index, carry):
        owner = owner_ref[index]
        line = (y + NY - (owner >> 4)) & (NY - 1)
        row = pl.multiple_of((line * NZ + ((owner >> 1) & (NZ - 1))) * SLICE, SLICE)
        target = pl.ds(pl.multiple_of(index * SLICE, SLICE), SLICE)
        here = (owner & 1) == core

        @pl.when(here)
        def _():
            out_ref[target, :] = mine_ref[pl.ds(row, SLICE), :]

        @pl.when(jnp.logical_not(here))
        def _():
            out_ref[target, :] = theirs_ref[pl.ds(row, SLICE), :]

        return carry

    lax.fori_loop(0, HMAX, one, 0)


def pick(place, owner, mine, theirs):
    return pl.pallas_call(
        pick_kernel,
        out_shape=jax.ShapeDtypeStruct((HMAX * SLICE, PADDED), BF16),
        in_specs=[SCALARS, SCALARS, WHOLE, WHOLE],
        out_specs=WHOLE,
        compiler_params=pltpu.CompilerParams(vmem_limit_bytes=8 * MIB),
        name="pick",
    )(place, owner, mine, theirs)


def norm_kernel(parts_ref, q_gain_ref, kv_gain_ref, cos_ref, sin_ref, after_ref, out_ref, row_ref):
    groups = NY * NC
    wide = COLS // groups
    for group in range(groups):
        total = parts_ref[group * NX]
        for other in range(1, NX):
            total = total + parts_ref[group * NX + other]
        row_ref[:, group * wide : (group + 1) * wide] = total
    query = row_ref[:, :QL]
    scale = lax.rsqrt(jnp.mean(query * query, axis=1, keepdims=True) + EPS)
    out_ref[:, :QL] = (query * scale * q_gain_ref[...]).astype(BF16)
    key = row_ref[:, QL : QL + KL]
    scale = lax.rsqrt(jnp.mean(key * key, axis=1, keepdims=True) + EPS)
    out_ref[:, QL : QL + KL] = (key * scale * kv_gain_ref[...]).astype(BF16)
    rope = rotate(row_ref[:, QL + KL :], cos_ref[...], sin_ref[...])
    out_ref[:, QL + KL :] = rope.astype(BF16)


def norm(parts, q_gain, kv_gain, cosine, sine, after):
    return pl.pallas_call(
        norm_kernel,
        out_shape=jax.ShapeDtypeStruct((QUART, COLS), BF16),
        in_specs=[WHOLE] * 5 + [OUTSIDE],
        out_specs=WHOLE,
        scratch_shapes=[pltpu.VMEM((QUART, COLS), F32)],
        compiler_params=pltpu.CompilerParams(vmem_limit_bytes=8 * MIB),
        name="norm",
    )(parts, q_gain, kv_gain, cosine, sine, after)


def query_kernel(norm_ref, w_ref, up_ref, cos_ref, sin_ref, after_ref, out_ref):
    query = jnp.dot(norm_ref[...], w_ref[...], preferred_element_type=F32).astype(BF16)
    for pair in range(2):
        base = pair * (ND + RD)
        lifted = jnp.dot(
            query[:, base : base + ND], up_ref[pair], preferred_element_type=F32
        )
        out_ref[pair, :, :KL] = lifted.astype(BF16)
        rope = query[:, base + ND : base + ND + RD].astype(F32)
        out_ref[pair, :, KL:WIDTH] = rotate(rope, cos_ref[...], sin_ref[...]).astype(BF16)
        lane = lax.broadcasted_iota(jnp.int32, (out_ref.shape[1], PADDED - WIDTH), 1)
        out_ref[pair, :, WIDTH:] = jnp.where(lane == 0, 1.0, 0.0).astype(BF16)


def queries(q_norm, w_qb, w_uk, cosine, sine, after):
    heads = w_uk.shape[0]
    rows = q_norm.shape[0]
    wide = 2 * (ND + RD)
    return pl.pallas_call(
        query_kernel,
        out_shape=jax.ShapeDtypeStruct((heads, rows, PADDED), BF16),
        grid=(heads // 2,),
        in_specs=[
            pl.BlockSpec((rows, QL), lambda i: (0, 0)),
            pl.BlockSpec((QL, wide), lambda i: (0, i)),
            pl.BlockSpec((2, ND, KL), lambda i: (i, 0, 0)),
            pl.BlockSpec((rows, RD), lambda i: (0, 0)),
            pl.BlockSpec((rows, RD), lambda i: (0, 0)),
            pl.BlockSpec(memory_space=pl.ANY),
        ],
        out_specs=pl.BlockSpec((2, rows, PADDED), lambda i: (i, 0, 0)),
        compiler_params=pltpu.CompilerParams(vmem_limit_bytes=GRANT),
        cost_estimate=pl.CostEstimate(
            flops=2 * rows * QL * QL, bytes_accessed=7 * MIB, transcendentals=0
        ),
        name="queries",
    )(q_norm, w_qb, w_uk, cosine, sine, after)


def move(pairs, sems):
    copies = [
        pltpu.make_async_copy(source, target, sems.at[index])
        for index, (source, target) in enumerate(pairs)
    ]
    for copy in copies:
        copy.start()
    for copy in copies:
        copy.wait()


def stack_kernel(*refs):
    out_ref = refs[-1]
    start = 0
    for ref in refs[:-1]:
        out_ref[pl.ds(start, ref.shape[0]), :] = ref[...]
        start += ref.shape[0]


def stack(*blocks):
    shape = (sum(b.shape[0] for b in blocks), blocks[0].shape[1])
    return pl.pallas_call(
        stack_kernel,
        out_shape=jax.ShapeDtypeStruct(shape, blocks[0].dtype),
        in_specs=[WHOLE] * len(blocks),
        out_specs=WHOLE,
        compiler_params=pltpu.CompilerParams(vmem_limit_bytes=16 * MIB),
        name="stack",
    )(*blocks)


def gate_kernel(*refs):
    del refs


def gate(blocks, *after):
    return pl.pallas_call(
        gate_kernel,
        out_shape=[jax.ShapeDtypeStruct(b.shape, b.dtype) for b in blocks],
        in_specs=[OUTSIDE] * (len(blocks) + len(after)),
        out_specs=[OUTSIDE] * len(blocks),
        input_output_aliases={i: i for i in range(len(blocks))},
        compiler_params=pltpu.CompilerParams(vmem_limit_bytes=4 * MIB),
        name="gate",
    )(*blocks, *after)


def project_kernel(place_ref, down_in, *refs):
    count = NY * NC
    blocks, (out_ref, token_ref, down_ref, sems) = refs[:count], refs[count:]
    pairs = [(down_in, down_ref)] + [(ref, token_ref.at[i]) for i, ref in enumerate(blocks)]
    copies = [
        pltpu.make_async_copy(source, target, sems.at[index])
        for index, (source, target) in enumerate(pairs)
    ]
    for copy in copies:
        copy.start()
    y, core = place_ref[0], place_ref[2]
    copies[0].wait()
    for index in range(count):
        copies[index + 1].wait()
        line = (y + NY - index // NC) & (NY - 1)
        side = core if index % NC == 0 else 1 - core
        out_ref[line, side] = jnp.dot(
            token_ref[index], down_ref[...], preferred_element_type=F32
        )


def project(place, blocks, down):
    rows = blocks[0].shape[0]
    return pl.pallas_call(
        project_kernel,
        out_shape=jax.ShapeDtypeStruct((NY, NC, rows, down.shape[1]), F32),
        in_specs=[SCALARS] + [OUTSIDE] * (len(blocks) + 1),
        out_specs=WHOLE,
        scratch_shapes=[
            pltpu.VMEM((len(blocks),) + blocks[0].shape, BF16),
            pltpu.VMEM(down.shape, BF16),
            pltpu.SemaphoreType.DMA((len(blocks) + 1,)),
        ],
        compiler_params=pltpu.CompilerParams(vmem_limit_bytes=GRANT),
        name="project",
    )(place, down, *blocks)


def spread_kernel(place_ref, normed_ref, after_ref, send_ref):
    x = place_ref[3]
    send_ref[:, WIDTH:] = jnp.zeros((send_ref.shape[0], PADDED - WIDTH), BF16)
    send_ref[:HALF, :WIDTH] = normed_ref[:HALF, QL:]
    first = pl.multiple_of(HALF + x * SIXTEENTH, SIXTEENTH)
    send_ref[HALF:, :WIDTH] = normed_ref[pl.ds(first, SIXTEENTH), QL:]


def spread(place, normed, after):
    return pl.pallas_call(
        spread_kernel,
        out_shape=jax.ShapeDtypeStruct((HALF + SIXTEENTH, PADDED), BF16),
        in_specs=[SCALARS, WHOLE, OUTSIDE],
        out_specs=WHOLE,
        compiler_params=pltpu.CompilerParams(vmem_limit_bytes=8 * MIB),
        name="spread",
    )(place, normed, after)


def split_kernel(line_ref, whole_ref, piece_ref):
    both = HALF + SIXTEENTH
    for index in range(NZ):
        start = index * both
        whole_ref[pl.ds(index * HALF, HALF), :] = line_ref[pl.ds(start, HALF), :]
        piece_ref[pl.ds(index * SIXTEENTH, SIXTEENTH), :] = line_ref[
            pl.ds(start + HALF, SIXTEENTH), :
        ]


def split(line):
    return pl.pallas_call(
        split_kernel,
        out_shape=[
            jax.ShapeDtypeStruct((NZ * HALF, PADDED), BF16),
            jax.ShapeDtypeStruct((NZ * SIXTEENTH, PADDED), BF16),
        ],
        in_specs=[WHOLE],
        out_specs=[WHOLE] * 2,
        compiler_params=pltpu.CompilerParams(vmem_limit_bytes=8 * MIB),
        name="split",
    )(line)


def hide(key_ref, first, size, hidden):
    lane = lax.broadcasted_iota(jnp.int32, (size, PADDED - WIDTH), 1)
    value = jnp.where((lane == 0) & hidden, NEGATIVE, 0.0)
    key_ref[pl.ds(first, size), WIDTH:] = value.astype(BF16)


def fold(state, query_at, key_ref, rows, first, masks):
    top_ref, sum_ref, acc_ref = state

    def score(start):
        return lax.dot_general(
            query_at(start), key_ref[...], (((1,), (1,)), ((), ())), preferred_element_type=F32
        )

    ready = score(0)
    for start in range(0, rows, GROUP):
        scores = ready
        if start + GROUP < rows:
            ready = score(start + GROUP)
        if masks:
            pieces, done = [], 0
            for begin, end, seen in masks:
                if begin > done:
                    pieces.append(scores[:, done:begin])
                pieces.append(jnp.where(seen, scores[:, begin:end], NEGATIVE))
                done = end
            if done < scores.shape[1]:
                pieces.append(scores[:, done:])
            scores = jnp.concatenate(pieces, axis=1)
        part = pl.ds(pl.multiple_of(first + start, GROUP), GROUP)
        top = jnp.max(scores, axis=1, keepdims=True)
        weights = jnp.exp2((scores - top) * LOG2)
        top_ref[part, :] = top
        sum_ref[part, :] = jnp.sum(weights, axis=1, keepdims=True)
        acc_ref[part, :] = jnp.dot(
            weights.astype(BF16), key_ref[:, :KL], preferred_element_type=F32
        )


def lift(side, w_ref, out_ref, top_ref, sum_ref, acc_ref):
    heads = w_ref.shape[0]
    for head in range(heads):
        part = pl.ds((side * heads + head) * CH, CH)
        mixed = acc_ref[part, :]
        high = mixed.astype(BF16)
        low = (mixed - high.astype(F32)).astype(BF16)
        weight = w_ref[head]
        halves = jnp.concatenate([high, low], axis=0)
        lifted = jnp.dot(halves, weight, preferred_element_type=F32)
        lifted = lifted[:CH] + lifted[CH:]
        out_ref[:, head * VD : (head + 1) * VD] = lifted
        at = heads * VD + head
        out_ref[:, at : at + 1] = top_ref[part, :]
        out_ref[:, at + heads : at + heads + 1] = sum_ref[part, :]


def prefix_kernel(place_ref, q_ref, key_in, w_ref, after_ref, out_ref, *scratch):
    top_ref, sum_ref, acc_ref, key_ref, sems = scratch
    state = (top_ref, sum_ref, acc_ref)
    rows = q_ref.shape[0]
    size = key_ref.shape[0] // NX
    move([(key_in, key_ref)], sems)
    for index in range(NX):
        for slot in range(HMAX):
            if slot >= LEAST:
                hide(key_ref, index * size + slot * SLICE, SLICE, slot >= place_ref[4])
    query_at = lambda start: q_ref[start : start + GROUP, :]
    fold(state, query_at, key_ref, rows, 0, ())
    lift(0, w_ref, out_ref, top_ref, sum_ref, acc_ref)


def state_scratch(rows):
    return [
        pltpu.VMEM((rows, 1), F32),
        pltpu.VMEM((rows, 1), F32),
        pltpu.VMEM((rows, KL), F32),
    ]


def lifted_shape(w_uv):
    return jax.ShapeDtypeStruct((CH, w_uv.shape[0] * VD + CH), F32)


def prefix_pass(place, query, keys, w_uv, after):
    rows = query.shape[0]
    return pl.pallas_call(
        prefix_kernel,
        out_shape=lifted_shape(w_uv),
        in_specs=[SCALARS, WHOLE, OUTSIDE, WHOLE, OUTSIDE],
        out_specs=WHOLE,
        scratch_shapes=state_scratch(rows)
        + [
            pltpu.VMEM(keys.shape, BF16),
            pltpu.SemaphoreType.DMA((1,)),
        ],
        compiler_params=pltpu.CompilerParams(vmem_limit_bytes=GRANT),
        cost_estimate=pl.CostEstimate(
            flops=2 * rows * keys.shape[0] * (WIDTH + KL),
            bytes_accessed=8 * MIB,
            transcendentals=rows * keys.shape[0],
        ),
        name="prefix",
    )(place, query, keys, w_uv, after)


def stretch_kernel(kinds, place_ref, q_ref, *refs):
    pieces, refs = refs[: len(kinds)], refs[len(kinds) :]
    w_ref, _, keep_ref, give_ref, top_ref, sum_ref, acc_ref, key_ref, sems = refs
    copies = []
    for index, ((kind, by), ref) in enumerate(zip(kinds, pieces)):
        if kind == "line" and by:
            line = (place_ref[0] + NY - by) & (NY - 1)
            ref = ref.at[pl.ds(pl.multiple_of(line * PIECE, PIECE), PIECE), :]
        target = key_ref.at[pl.ds(index * PIECE, PIECE), :]
        copies.append(pltpu.make_async_copy(ref, target, sems.at[index]))
        copies[-1].start()
    y, z, core, x = (place_ref[i] for i in range(4))
    span = (y * NZ + z) * NC + core
    for copy in copies:
        copy.wait()
    mixed = []
    for index, (kind, by) in enumerate(kinds):
        start = index * PIECE
        if kind == "line" and by:
            hide(key_ref, start, PIECE, by > y)
        elif kind == "line":
            lane = lax.broadcasted_iota(jnp.int32, (1, PIECE), 1)
            mixed.append((start, start + PIECE, lane // HALF, lane % HALF))
        else:
            size = NZ * SIXTEENTH
            for line in range(1, NY):
                hide(key_ref, start + line * size, size, line > y)
            lane = lax.broadcasted_iota(jnp.int32, (1, size), 1)
            token = HALF + SIXTEENTH * ((x + NX - by) & (NX - 1)) + lane % SIXTEENTH
            mixed.append((start, start + size, lane // SIXTEENTH, token))
    rows = q_ref.shape[0] // 2

    def side_pass(side, carry):
        base = (span + side * (1 - 2 * core)) * CH
        own = lax.broadcasted_iota(jnp.int32, (GROUP, 1), 0) % CH + base
        masks = [
            (begin, end, ((y * NZ + column) * NC + core) * CH + token <= own)
            for begin, end, column, token in mixed
        ]

        def query_at(start):
            return q_ref[pl.ds(pl.multiple_of(side * rows + start, GROUP), GROUP), :]

        fold((top_ref, sum_ref, acc_ref), query_at, key_ref, rows, side * rows, masks)
        return carry

    lax.fori_loop(0, NC, side_pass, 0)
    lift(0, w_ref, keep_ref, top_ref, sum_ref, acc_ref)
    lift(1, w_ref, give_ref, top_ref, sum_ref, acc_ref)


def stretch_pass(place, query, pieces, w_uv, after):
    rows = query.shape[0]
    kinds = tuple(piece[:2] for piece in pieces)
    arrays = [piece[2] for piece in pieces]
    keys = len(kinds) * PIECE
    operands = [place, query, *arrays, w_uv, after]
    return pl.pallas_call(
        functools.partial(stretch_kernel, kinds),
        out_shape=[lifted_shape(w_uv)] * 2,
        in_specs=[SCALARS, WHOLE] + [OUTSIDE] * len(kinds) + [WHOLE, OUTSIDE],
        out_specs=[WHOLE] * 2,
        scratch_shapes=state_scratch(rows)
        + [
            pltpu.VMEM((keys, PADDED), BF16),
            pltpu.SemaphoreType.DMA((len(kinds),)),
        ],
        compiler_params=pltpu.CompilerParams(vmem_limit_bytes=GRANT),
        cost_estimate=pl.CostEstimate(
            flops=2 * rows * keys * (WIDTH + KL),
            bytes_accessed=8 * MIB,
            transcendentals=rows * keys,
        ),
        name="stretch",
    )(*operands)


def merge_kernel(*refs):
    parts, out_ref = refs[:-1], refs[-1]
    heads = out_ref.shape[1] // VD
    for head in range(heads):
        at = heads * VD + head
        tops = [ref[:, at : at + 1] for ref in parts]
        top = functools.reduce(jnp.maximum, tops)
        total = mixed = 0.0
        for ref, own in zip(parts, tops):
            scale = jnp.exp2((own - top) * LOG2)
            total = total + ref[:, at + heads : at + heads + 1] * scale
            mixed = mixed + ref[:, head * VD : (head + 1) * VD] * scale
        out_ref[:, head * VD : (head + 1) * VD] = (mixed / total).astype(BF16)


def merge(parts):
    return pl.pallas_call(
        merge_kernel,
        out_shape=jax.ShapeDtypeStruct((CH, parts[0].shape[1] - CH), BF16),
        in_specs=[WHOLE] * len(parts),
        out_specs=WHOLE,
        compiler_params=pltpu.CompilerParams(vmem_limit_bytes=12 * MIB),
        name="merge",
    )(*parts)


def body(
    hidden_in,
    w_down,
    q_gain,
    kv_gain,
    w_qb,
    w_uk,
    w_uv,
    cache_pool,
    hit_owner,
    hit_block,
    hit_count,
):
    y = lax.axis_index("y").astype(jnp.int32)
    z = lax.axis_index("z").astype(jnp.int32)
    c = lax.axis_index("c").astype(jnp.int32)
    x = lax.axis_index("x").astype(jnp.int32)
    span = (y * NZ + z) * NC + c
    my_owner = lax.dynamic_index_in_dim(hit_owner, span, 0, keepdims=False)
    my_count = lax.dynamic_index_in_dim(hit_count, span, 0, keepdims=False)
    place = jnp.stack([y, z, c, x, my_count])
    rows = hidden_in.shape[0]
    heads = w_uk.shape[0]
    feats = hidden_in.shape[1]
    parts = NY * NC
    per = w_down.shape[0]
    wide = COLS // parts
    cosine, sine = rope_tables(span * CH + jnp.arange(rows, dtype=jnp.int32))
    quarter = lambda table: lax.dynamic_slice_in_dim(table, x * QUART, QUART, 0)

    pair = NC * per
    hidden = hidden_in.reshape(rows, NY, NZ, pair).transpose(0, 2, 1, 3).reshape(rows, feats)
    pieces = w_down.reshape(per, parts, wide).transpose(1, 0, 2)
    pieces = lax.all_to_all(pieces, ("y", "c"), 0, 0, tiled=True).reshape(parts * per, wide)
    down = lax.all_gather(pieces, "z", axis=0, tiled=True)
    (hidden,) = gate([hidden], pieces, cosine, sine)
    others = gate(offsets(hidden, "y", NY)[1:], down)
    tokens = []
    for block in [hidden, *others]:
        tokens += [block, shift(block, "c", NC, 1)]

    pool = lax.all_gather(quarter_pool(x, cache_pool), "z", axis=0, tiled=True)
    table = lambda array: lax.dynamic_index_in_dim(
        array.reshape(NY, NZ, NC, -1), z, 1, keepdims=False
    )
    live = jnp.arange(HMAX, dtype=jnp.int32) < table(hit_count)
    owners = (y * NZ + jnp.arange(NZ, dtype=jnp.int32)) * NC + c
    asking = (table(hit_owner) == owners[:, None, None, None]) & live
    wanted = jnp.sum(jnp.where(asking, table(hit_block), 0), axis=3)
    wanted = wanted + PB * jnp.arange(NZ, dtype=jnp.int32)[:, None, None]
    wanted = jnp.transpose(wanted, (1, 2, 0)).reshape(-1)
    partial_proj = project(place, tokens, down).reshape(parts * rows, wide)
    arrived = lax.all_to_all(partial_proj, ("y", "c", "x"), 0, 0, tiled=True)
    served = serve(place, wanted, pool, arrived)
    served = [served[0]] + [shift(served[by], "y", NY, by) for by in range(1, NY)]

    normed = norm(
        arrived.reshape(parts * NX, QUART, wide),
        q_gain[None, :],
        kv_gain[None, :],
        quarter(cosine),
        quarter(sine),
        served[0],
    )
    normed = lax.all_gather(normed, "x", axis=0, tiled=True)
    ours, give = sort(served)
    send = spread(place, normed, ours)

    whole, piece = split(lax.all_gather(send, "z", axis=0, tiled=True))
    piece = stack(*offsets(piece, "y", NY))
    lines = lax.all_gather(whole, "y", axis=0, tiled=True)
    planes = offsets(piece, "x", NX)
    prefix = pick(place, my_owner, ours, shift(give, "c", NC, 1))
    prefix_all = lax.all_gather(prefix, "x", axis=0, tiled=True)

    query = queries(normed, w_qb, w_uk, cosine, sine, piece).reshape(heads * rows, PADDED)
    query_all = stack(query, shift(query, "c", NC, 1))

    parts = []
    for pieces in (
        [("line", 0, whole), ("plane", 0, planes[0])],
        [("line", by, lines) for by in (1, 2, 3)],
        [("plane", by, planes[by]) for by in (1, 3, 2)],
    ):
        keep, give = stretch_pass(place, query_all, pieces, w_uv, parts[-2] if parts else piece)
        parts += [keep, shift(give, "c", NC, 1)]
    parts.append(prefix_pass(place, query, prefix_all, w_uv, parts[-2]))
    return merge(parts)


def solution(mesh):
    fine = Mesh(mesh.devices.reshape(NY, NZ, NC, NX), ("y", "z", "c", "x"))
    span = SPAN_AXES
    in_specs = (
        P(span, "x"),
        P(("x",) + span, None),
        P(),
        P(),
        P(None, "x"),
        P("x", None, None),
        P("x", None, None),
        P(span, None, None),
        P(),
        P(),
        P(),
    )
    return jax.shard_map(
        body, mesh=fine, in_specs=in_specs, out_specs=P(span, "x"), check_vma=False
    )
```
